768 devices in a mesh: gx: 96 (over z, y), gy: 8 (over x, core).
Axes of the slice: x: 4, y: 8, z: 12, core: 2. Of those that a mesh axis runs over, the one named last changes fastest.
Arguments:
- fine_state: float32 [1536, 5, 32, 1024], P(('gx', 'gy')), may hold values from -2 to 8, as said below
- fine_links: int32 [1536, 2, 5], P(('gx', 'gy')), may hold values from 0 to 3, as said below
- coarse_edges: float32 [768, 2, 5, 2, 1024], P(('gx', 'gy')), may hold values from -2 to 8, as said below
- flux_register: float32 [768, 2, 5, 1024], P(('gx', 'gy')), may hold values from -8 to 8
Outputs:
- fine_new: float32 [1536, 5, 32, 1024], P(('gx', 'gy'))
- coarse_faces: float32 [768, 2, 5, 1024], P(('gx', 'gy'))
The draws below stay inside these ranges and needn't reach their ends.
Inputs may be any that keep to these rules, and one draw needn't show every extreme that they name: `fine_state`: conserved states (density, three momenta, total energy) of an ideal gas with ratio of specific heats 1.4: in every cell density and pressure lie in 1 to 2 and each velocity component in -1 to 1. `coarse_edges`: as fine_state: density and pressure 1 to 2, velocity components -1 to 1 in every cell. `fine_links`: columns: kind (0 a fine neighbour, 1 a coarse block), row offset plus one (0 to 2), column offset plus one (0 to 2, always 1 where kind is 1), slot (below 2 where kind is 0, below 1 where kind is 1), quadrant (0 to 3). The first block of every device has kind 1 on both sides, with row offset plus one 2 on its low side and 0 on its high side; the second block of every device has kind 0 on both sides, with row offset plus one 0 on its low side and 2 on its high side.
All inputs are finite; a program needn't handle non-finite values.
Results may differ from the reference program's by a relative error of at most 0.0003.
Values sent between devices are 32-bit elements; how exact they have to be, the bound alone decides.
A program may use at most 32 MiB of HBM per device.

```python
import jax
import jax.numpy as jnp
from jax import lax

B = 32
FIELDS = 5
FB = 2
CB = 1
NFINE = 1536
NCOARSE = 768
N_GX = 96
N_GY = 8


def gas_state(key, shape, axis, power):
    streams = jax.random.split(key, 5)
    density = 1.0 + jax.random.uniform(streams[0], shape, jnp.float32) ** power
    speed_x = jax.random.uniform(streams[1], shape, jnp.float32, -1.0, 1.0)
    speed_y = jax.random.uniform(streams[2], shape, jnp.float32, -1.0, 1.0)
    speed_z = jax.random.uniform(streams[3], shape, jnp.float32, -1.0, 1.0)
    pressure = 1.0 + jax.random.uniform(streams[4], shape, jnp.float32) ** power
    energy = pressure / 0.4 + 0.5 * density * (speed_x * speed_x + speed_y * speed_y + speed_z * speed_z)
    return jnp.stack([density, density * speed_x, density * speed_y, density * speed_z, energy], axis=axis)


def draw_fine_state(key, part):
    key = jax.random.fold_in(key, 11)
    power = 1.0
    return gas_state(key, (NFINE, B, B * B), 1, power)


def draw_coarse_edges(key, part):
    key = jax.random.fold_in(key, 23)
    power = 1.0
    return gas_state(key, (NCOARSE, 2, 2, B * B), 2, power)


def draw_fine_links(key, part):
    key = jax.random.fold_in(key, 37)
    streams = jax.random.split(key, 6)
    shape = (NFINE, 2)
    position = jnp.arange(NFINE, dtype=jnp.int32) % FB
    first_block = (position == 0)[:, None]
    second_block = (position == 1)[:, None]
    first_rows = jnp.array([[2, 0]], jnp.int32)
    second_rows = jnp.array([[0, 2]], jnp.int32)
    random_kind = (jax.random.randint(streams[0], shape, 0, 4) == 0).astype(jnp.int32)
    link_kind = jnp.where(first_block, 1, jnp.where(second_block, 0, random_kind))
    random_row = jax.random.randint(streams[1], shape, 0, 3)
    offset_row = jnp.where(first_block, first_rows, jnp.where(second_block, second_rows, random_row))
    offset_col = jnp.where(link_kind == 1, 1, jax.random.randint(streams[2], shape, 0, 3))
    slot_index = jnp.where(link_kind == 1, jax.random.randint(streams[3], shape, 0, CB), jax.random.randint(streams[4], shape, 0, FB))
    quadrant = jax.random.randint(streams[5], shape, 0, 4)
    return jnp.stack([link_kind, offset_row, offset_col, slot_index, quadrant], axis=-1).astype(jnp.int32)


def block_scale(rng, dims, cuts, least, largest):
    def one(dim, blocks):
        steps = jax.random.uniform(jax.random.fold_in(jax.random.fold_in(rng, 6), dim), (blocks,), jnp.float32, least / len(cuts), largest / len(cuts))
        return jnp.repeat(jnp.exp(steps), dims[dim] // blocks).reshape((-1,) + (1,) * (len(dims) - dim - 1))

    factor_of = one(*cuts[0])
    for cut in cuts[1:]:
        factor_of = factor_of * one(*cut)
    return factor_of


def bell_draw(key, shape, scale, limit, cuts=(), kind=jnp.bfloat16):
    values = jax.random.normal(key, shape, jnp.float32) * scale
    if len(cuts) > 0:
        values = block_scale(key, shape, cuts, -0.22, 0.18) * values
    return jnp.clip(values, min=-limit, max=limit).astype(kind)


def setup_inputs(seed: int = 0) -> dict:
    seeds = jax.random.split(jax.random.key(seed), 5)
    return {
        "fine_state": draw_fine_state(jax.random.fold_in(seeds[4], 71), 0),
        "fine_links": draw_fine_links(jax.random.fold_in(seeds[4], 71), 0),
        "coarse_edges": draw_coarse_edges(jax.random.fold_in(seeds[4], 71), 0),
        "flux_register": bell_draw(seeds[3], (NCOARSE, 2, FIELDS, B * B), 2.0, 8.0, ((0, 768),), jnp.float32),
    }


ADIABATIC = 1.4
FINE_RATIO = 0.1
COARSE_RATIO = 0.05

def primitives(conserved):
    density = conserved[0]
    speed_x = conserved[1] / density
    speed_y = conserved[2] / density
    speed_z = conserved[3] / density
    kinetic = 0.5 * density * (speed_x * speed_x + speed_y * speed_y + speed_z * speed_z)
    pressure = (ADIABATIC - 1.0) * (conserved[4] - kinetic)
    return jnp.stack([density, speed_x, speed_y, speed_z, pressure])

def face_states(primitive):
    extent = primitive.shape[1]
    edge_values = 7.0 / 12.0 * (primitive[:, 1:extent - 2] + primitive[:, 2:extent - 1]) - 1.0 / 12.0 * (primitive[:, 0:extent - 3] + primitive[:, 3:extent])
    middle = primitive[:, 2:extent - 2]
    lower_edge = edge_values[:, 0:extent - 4]
    upper_edge = edge_values[:, 1:extent - 3]
    slope_diff = upper_edge - lower_edge
    curvature = 6.0 * (middle - 0.5 * (lower_edge + upper_edge))
    sound_speed = jnp.sqrt(ADIABATIC * middle[4] / middle[0])
    reach_up = FINE_RATIO * jnp.maximum(middle[1] + sound_speed, 0.0)
    reach_down = FINE_RATIO * jnp.maximum(sound_speed - middle[1], 0.0)
    upper_state = upper_edge - 0.5 * reach_up * (slope_diff - (1.0 - 2.0 / 3.0 * reach_up) * curvature)
    lower_state = lower_edge + 0.5 * reach_down * (slope_diff + (1.0 - 2.0 / 3.0 * reach_down) * curvature)
    return (upper_state[:, :-1], lower_state[:, 1:])

def describe(state):
    density = state[0]
    speed_x = state[1]
    pressure = state[4]
    energy = pressure / (ADIABATIC - 1.0) + 0.5 * density * (speed_x * speed_x + state[2] * state[2] + state[3] * state[3])
    conserved = jnp.stack([density, density * speed_x, density * state[2], density * state[3], energy])
    physical = jnp.stack([density * speed_x, density * speed_x * speed_x + pressure, density * speed_x * state[2], density * speed_x * state[3], speed_x * (energy + pressure)])
    sound_speed = jnp.sqrt(ADIABATIC * pressure / density)
    return (energy, conserved, physical, sound_speed)

def hllc_flux(left_state, right_state):
    left_energy, left_cons, left_phys, left_sound = describe(left_state)
    right_energy, right_cons, right_phys, right_sound = describe(right_state)
    wave_left = jnp.minimum(left_state[1] - left_sound, right_state[1] - right_sound)
    wave_right = jnp.maximum(left_state[1] + left_sound, right_state[1] + right_sound)
    mass_left = left_state[0] * (wave_left - left_state[1])
    mass_right = right_state[0] * (wave_right - right_state[1])
    contact = (right_state[4] - left_state[4] + mass_left * left_state[1] - mass_right * right_state[1]) / (mass_left - mass_right)

    def star_flux(state, energy, conserved, physical, mass, wave):
        factor = mass / (wave - contact)
        star = factor * jnp.stack([jnp.ones_like(contact), contact, state[2], state[3], energy / state[0] + (contact - state[1]) * (contact + state[4] / mass)])
        return physical + wave * (star - conserved)
    star_left = star_flux(left_state, left_energy, left_cons, left_phys, mass_left, wave_left)
    star_right = star_flux(right_state, right_energy, right_cons, right_phys, mass_right, wave_right)
    return jnp.where(wave_left >= 0.0, left_phys, jnp.where(contact >= 0.0, star_left, jnp.where(wave_right > 0.0, star_right, right_phys)))

def advance_block(extended):
    primitive = primitives(extended)
    upper_state, lower_state = face_states(primitive)
    flux = hllc_flux(upper_state, lower_state)
    interior = extended[:, 3:-3]
    updated = interior - FINE_RATIO * (flux[:, 1:] - flux[:, :-1])
    return (updated, jnp.stack([flux[:, 0], flux[:, -1]]))

def prolong(source, quadrant, low_side, width):
    fields = source.shape[0]
    grid = source.reshape(fields, 2, width, width)
    half = width // 2
    row_start = (quadrant // 2 * half).astype(jnp.int32)
    col_start = (quadrant % 2 * half).astype(jnp.int32)
    anchor = jnp.zeros((), jnp.int32)
    corner = lax.dynamic_slice(grid, (anchor, anchor, row_start, col_start), (fields, 2, half, half))
    spread = jnp.repeat(jnp.repeat(corner, 2, axis=2), 2, axis=3).reshape(fields, 2, width * width)
    if low_side:
        return jnp.stack([spread[:, 1], spread[:, 0], spread[:, 0]], axis=1)
    return jnp.stack([spread[:, 0], spread[:, 0], spread[:, 1]], axis=1)

def place_patch(face_row, quadrant, width):
    fields = face_row.shape[0]
    half = width // 2
    averaged = face_row.reshape(fields, half, 2, half, 2).mean(axis=(2, 4))
    row_start = (quadrant // 2 * half).astype(jnp.int32)
    col_start = (quadrant % 2 * half).astype(jnp.int32)
    anchor = jnp.zeros((), jnp.int32)
    placed = lax.dynamic_update_slice(jnp.zeros((fields, width, width), jnp.float32), averaged, (anchor, row_start, col_start))
    return 0.5 * placed.reshape(fields, width * width)

def reference(fine_state, fine_links, coarse_edges, flux_register):
    width = fine_state.shape[2]
    fields = fine_state.shape[1]

    def one_block(index):
        device = index // FB
        row_gx = device // N_GY
        col_gy = device % N_GY
        ghosts = []
        for which_side in (0, 1):
            link = fine_links[index, which_side]
            near_gx = (row_gx + link[1] - 1) % N_GX
            near_gy = (col_gy + link[2] - 1) % N_GY
            fine_owner = (near_gx * N_GY + near_gy) * FB + jnp.minimum(link[3], FB - 1)
            coarse_owner = (near_gx * N_GY + col_gy) * CB + jnp.minimum(link[3], CB - 1)
            neighbour = fine_state[fine_owner]
            if which_side == 0:
                from_fine = neighbour[:, width - 3:]
            else:
                from_fine = neighbour[:, :3]
            from_coarse = prolong(coarse_edges[coarse_owner, 1 - which_side], link[4], which_side == 0, width)
            ghosts.append(jnp.where(link[0] == 1, from_coarse, from_fine))
        extended = jnp.concatenate([ghosts[0], fine_state[index], ghosts[1]], axis=1)
        return advance_block(extended)
    updated, face_flux = lax.map(one_block, jnp.arange(NFINE, dtype=jnp.int32))
    links_flat = fine_links.reshape(NFINE * 2, 5)
    block_index = jnp.repeat(jnp.arange(NFINE, dtype=jnp.int32), 2)
    side_index = jnp.tile(jnp.array([0, 1], jnp.int32), NFINE)
    device = block_index // FB
    row_gx = device // N_GY
    col_gy = device % N_GY
    near_gx = (row_gx + links_flat[:, 1] - 1) % N_GX
    target = ((near_gx * N_GY + col_gy) * CB + jnp.minimum(links_flat[:, 3], CB - 1)) * 2 + (1 - side_index)

    def patch_row(face_row, quadrant):
        return place_patch(face_row, quadrant, width)
    patches = jax.vmap(patch_row)(face_flux.reshape(NFINE * 2, fields, width * width), links_flat[:, 4])
    patches = patches * (links_flat[:, 0] == 1).astype(jnp.float32)[:, None, None]
    totals = jax.ops.segment_sum(patches, target, num_segments=NCOARSE * 2).reshape(NCOARSE, 2, fields, width * width)
    orient = jnp.array([1.0, -1.0], jnp.float32)[None, :, None, None]
    coarse_faces = coarse_edges[:, :, :, 0] + COARSE_RATIO * orient * (flux_register + totals)
    return (updated, coarse_faces)
```

```python
import jax
import jax.numpy as jnp
from jax import lax
from jax.experimental import pallas as pl
from jax.experimental.pallas import tpu as pltpu
from jax.sharding import PartitionSpec as P

MESH = pl.DeviceIdType.MESH
FIELDS = 5
ROWS, LANES = 8, 128


def plane_rows(x):
    return pl.ds((x // 8) * 64 + x % 8, ROWS, stride=8)


def load_plane(ref, block, x):
    return [ref[block, f, plane_rows(x), :] for f in range(FIELDS)]


def primitive(cell):
    rho, mx, my, mz, energy = cell
    inverse = 1.0 / rho
    u, v, w = mx * inverse, my * inverse, mz * inverse
    p = 0.4 * (energy - 0.5 * (mx * u + my * v + mz * w))
    return [rho, u, v, w, p, inverse]


def edge(w0, w1, w2, w3):
    return [
        (7.0 / 12.0) * (w1[f] + w2[f]) - (1.0 / 12.0) * (w0[f] + w3[f]) for f in range(FIELDS)
    ]


def square_root(x):
    return jnp.sqrt(x)


def states(w, low, high):
    u = w[1]
    c = square_root(1.4 * w[4] * w[5])
    up = 0.1 * jnp.maximum(u + c, 0.0)
    down = 0.1 * jnp.maximum(c - u, 0.0)
    half_up, keep_up = 0.5 * up, 1.0 - (2.0 / 3.0) * up
    half_down, keep_down = 0.5 * down, 1.0 - (2.0 / 3.0) * down
    upper, lower = [], []
    for f in range(FIELDS):
        diff = high[f] - low[f]
        curve = 6.0 * w[f] - 3.0 * (low[f] + high[f])
        upper.append(high[f] - half_up * (diff - keep_up * curve))
        lower.append(low[f] + half_down * (diff + keep_down * curve))
    return upper, lower


def hllc(left, right):
    rho_l, u_l, v_l, w_l, p_l = left
    rho_r, u_r, v_r, w_r, p_r = right
    t_l, t_r = p_l / rho_l, p_r / rho_r
    c_l, c_r = square_root(1.4 * t_l), square_root(1.4 * t_r)
    s_l = jnp.minimum(u_l - c_l, u_r - c_r)
    s_r = jnp.maximum(u_l + c_l, u_r + c_r)
    m_l, m_r = rho_l * (s_l - u_l), rho_r * (s_r - u_r)
    contact = (p_r - p_l + m_l * u_l - m_r * u_r) / (m_l - m_r)
    is_left = jnp.maximum(s_l, contact) >= 0.0

    def pick(a, b):
        return jnp.where(is_left, a, b)

    u, v, w, p, t = (pick(a, b) for a, b in zip((u_l, v_l, w_l, p_l, t_l), (u_r, v_r, w_r, p_r, t_r)))
    m, s = pick(m_l, m_r), pick(s_l, s_r)
    star = pick(-s_l, s_r) > 0.0
    speed = jnp.where(star, contact, u)
    inverse = 1.0 / (s - speed)
    mass = m * inverse * speed
    gap = speed - u
    pressure = p + m * gap
    kinetic = 0.5 * (u * u + v * v + w * w)
    return [
        mass,
        mass * speed + pressure,
        mass * v,
        mass * w,
        mass * (2.5 * t + kinetic + gap * speed) + speed * (gap * p * inverse + pressure),
    ]


def three_fluxes(w):
    a = [edge(w[i], w[i + 1], w[i + 2], w[i + 3]) for i in range(5)]
    sides = [states(w[i + 2], a[i], a[i + 1]) for i in range(4)]
    return [hllc(sides[i][0], sides[i + 1][1]) for i in range(3)]


def iotas():
    return (
        lax.broadcasted_iota(jnp.int32, (ROWS, LANES), 0),
        lax.broadcasted_iota(jnp.int32, (ROWS, LANES), 1),
    )


def prolong(value, q):
    row, lane = iotas()
    rows = (q // 2) * 4 + row // 2
    lanes = ((row % 2) * 2 + lane // 64) * 32 + (q % 2) * 16 + (lane % 32) // 2
    return jnp.take_along_axis(jnp.take_along_axis(value, rows, axis=0), lanes, axis=1)


def patch(flux, q):
    row, lane = iotas()
    total = flux + pltpu.roll(flux, LANES - 1, 1)
    total = total + pltpu.roll(total, LANES - 32, 1)
    lanes = ((lane // 32) % 2) * 64 + 2 * (lane % 16)
    rows = 2 * (row % 4) + lane // 64
    placed = jnp.take_along_axis(jnp.take_along_axis(total, lanes, axis=1), rows, axis=0)
    inside = (row // 4 == q // 2) & ((lane % 32) // 16 == q % 2)
    return jnp.where(inside, 0.125 * placed, 0.0)


def kernel(
    n_gx, n_gy, links, fine, coarse, register, out, faces_out,
    cells, own_coarse, own_register, low_faces, high_faces,
    from_below, from_above, coarse_below, coarse_above,
    flux_out, flux_below, flux_above, kept,
    local_sem, send_sem, recv_sem,
):
    gx, gy = lax.axis_index("gx"), lax.axis_index("gy")
    above = (lax.rem(gx + 1, n_gx), gy)
    below = (lax.rem(gx + n_gx - 1, n_gx), gy)
    right = (gx, lax.rem(gy + 1, n_gy))
    left = (gx, lax.rem(gy + n_gy - 1, n_gy))

    def fetch(src, dst, k):
        copy = pltpu.make_async_copy(src, dst, local_sem.at[k])
        copy.start()
        return copy

    def rows(ref, start, size):
        return ref.at[:, :, pl.ds(start, size), :]

    edges = [fetch(rows(fine, s, 64), rows(cells, s, 64), k) for k, s in enumerate((0, 192))]
    middle = fetch(rows(fine, 64, 128), rows(cells, 64, 128), 2)
    coarse_in = fetch(coarse, own_coarse, 3)
    register_in = fetch(register, own_register, 4)

    barrier = pltpu.get_barrier_semaphore()
    for device in (above, below, right, left):
        pl.semaphore_signal(barrier, inc=1, device_id=device, device_id_type=MESH)
    pl.semaphore_wait(barrier, 4)

    def send(src, dst, device, k):
        copy = pltpu.make_async_remote_copy(
            src_ref=src, dst_ref=dst, send_sem=send_sem.at[k], recv_sem=recv_sem.at[k],
            device_id=device, device_id_type=MESH,
        )
        copy.start()
        return copy

    sent = []
    coarse_up = send(coarse.at[0], coarse_below, above, 0)
    coarse_down = send(coarse.at[1], coarse_above, below, 1)

    for copy in edges:
        copy.wait()
    for b in range(2):
        for f in range(FIELDS):
            for x in range(3):
                low_faces[b, f, x] = cells[b, f, plane_rows(x), :]
                high_faces[b, f, x] = cells[b, f, plane_rows(29 + x), :]
    fine_up, fine_down = [], []
    for b in range(2):
        fine_up.append(send(high_faces.at[b], from_below.at[1, b], above, 2 + b))
        fine_down.append(send(low_faces.at[b], from_above.at[1, b], below, 4 + b))

    def block_edge(block, side, ghosts):
        if side == 0:
            inner = [load_plane(cells, block, x) for x in range(5)]
            w = [primitive(c) for c in inner]
            fluxes = three_fluxes(ghosts + w)
            targets = (0, 1)
        else:
            inner = [load_plane(cells, block, x) for x in range(27, 32)]
            w = [primitive(c) for c in inner]
            fluxes = three_fluxes(w + ghosts)
            targets = (3, 4)
        for k, i in enumerate(targets):
            for f in range(FIELDS):
                x = i if side == 0 else 27 + i
                out[block, f, plane_rows(x), :] = inner[i][f] - 0.1 * (
                    fluxes[k + 1][f] - fluxes[k][f]
                )
        return (fluxes[0], fluxes[2]) if side == 0 else (fluxes[2], fluxes[0])

    coarse_up.wait_recv()
    coarse_down.wait_recv()
    flux_sends = []
    for side in range(2):
        q = links[0, side, 4]
        source = coarse_above if side == 0 else coarse_below
        layers = [
            primitive([
                prolong(source[f, pl.ds(layer, ROWS, stride=2), :], q) for f in range(FIELDS)
            ])
            for layer in range(2)
        ]
        near, far = layers
        ghosts = [far, near, near] if side == 0 else [near, near, far]
        outer, inner = block_edge(0, side, ghosts)
        for f in range(FIELDS):
            flux_out[side, f] = patch(outer[f], q)
            kept[0, side, f] = inner[f]
        if side == 0:
            flux_sends.append(send(flux_out.at[0], flux_below, above, 14))
        else:
            flux_sends.append(send(flux_out.at[1], flux_above, below, 15))

    middle.wait()

    def bulk(block):
        first = [load_plane(cells, block, x) for x in range(6)]
        w = [primitive(c) for c in first]
        a = [edge(w[i], w[i + 1], w[i + 2], w[i + 3]) for i in range(3)]
        upper2, _ = states(w[2], a[0], a[1])
        upper3, lower3 = states(w[3], a[1], a[2])
        flux3 = hllc(upper2, lower3)
        for f in range(FIELDS):
            kept[block, 2, f] = flux3[f]

        def step(i, carry):
            w0, w1, w2, low, upper, flux = carry
            w3 = primitive(load_plane(cells, block, i + 2))
            high = edge(w0, w1, w2, w3)
            next_upper, lower = states(w1, low, high)
            next_flux = hllc(upper, lower)
            here = plane_rows(i - 1)
            for f in range(FIELDS):
                out[block, f, here, :] = cells[block, f, here, :] - 0.1 * (next_flux[f] - flux[f])
            return w1, w2, w3, high, next_upper, next_flux

        carry = (w[3], w[4], w[5], a[2], upper3, flux3)
        carry = lax.fori_loop(0, 13, lambda k, c: step(5 + 2 * k, step(4 + 2 * k, c)), carry)
        for f in range(FIELDS):
            kept[block, 3, f] = carry[5][f]

    forwards = []
    for b in range(2):
        bulk(b)
        for k, (near, ref) in enumerate(((fine_up[b], from_below), (fine_down[b], from_above))):
            near.wait_recv()
            base = 6 + 4 * b + 2 * k
            forwards.append(send(ref.at[1, b], ref.at[0, b], right, base))
            forwards.append(send(ref.at[1, b], ref.at[2, b], left, base + 1))

    for x, side, first, second in ((2, 0, 0, 2), (29, 1, 3, 1)):
        for f in range(FIELDS):
            here = plane_rows(x)
            out[0, f, here, :] = cells[0, f, here, :] - 0.1 * (
                kept[0, 2 if side == 0 else 1, f] - kept[0, 0 if side == 0 else 3, f]
            )

    coarse_in.wait()
    register_in.wait()
    for copy in flux_sends:
        copy.wait_recv()
    for t in range(2):
        sums = flux_above if t == 0 else flux_below
        factor = 0.05 if t == 0 else -0.05
        for f in range(FIELDS):
            here = pl.ds(t, ROWS, stride=2)
            faces_out[f, here, :] = own_coarse[t, f, pl.ds(0, ROWS, stride=2), :] + factor * (
                own_register[f, here, :] + sums[f]
            )

    for copy in forwards:
        copy.wait_recv()
    for side in (1, 0):
        ref = from_below if side == 0 else from_above
        column, slot = links[1, side, 2], links[1, side, 3]
        ghosts = [
            primitive([ref[column, slot, f, x] for f in range(FIELDS)]) for x in range(3)
        ]
        _, inner = block_edge(1, side, ghosts)
        x = 2 if side == 0 else 29
        here = plane_rows(x)
        for f in range(FIELDS):
            if side == 0:
                change = kept[1, 2, f] - inner[f]
            else:
                change = inner[f] - kept[1, 3, f]
            out[1, f, here, :] = cells[1, f, here, :] - 0.1 * change

    for copy in [coarse_up, coarse_down] + fine_up + fine_down + flux_sends + forwards:
        copy.wait_send()


def shards(fine_state, fine_links, coarse_edges, flux_register):
    n_gx, n_gy = lax.axis_size("gx"), lax.axis_size("gy")
    f32 = jnp.float32
    fine = fine_state.reshape(2, FIELDS, 4, 8, 8, LANES).transpose(0, 1, 2, 4, 3, 5)
    fine = fine.reshape(2, FIELDS, 256, LANES)
    coarse = coarse_edges.reshape(2, FIELDS, 2, 8, LANES).transpose(0, 1, 3, 2, 4)
    coarse = coarse.reshape(2, FIELDS, 16, LANES)
    register = flux_register.reshape(2, FIELDS, 8, LANES).transpose(1, 2, 0, 3)
    register = register.reshape(FIELDS, 16, LANES)
    plane = (ROWS, LANES)
    updated, faces = pl.pallas_call(
        lambda *refs: kernel(n_gx, n_gy, *refs),
        out_shape=[
            pltpu.VMEM((2, FIELDS, 256, LANES), f32),
            pltpu.VMEM((FIELDS, 16, LANES), f32),
        ],
        in_specs=[
            pl.BlockSpec(memory_space=pltpu.SMEM),
            pl.BlockSpec(memory_space=pltpu.HBM),
            pl.BlockSpec(memory_space=pltpu.HBM),
            pl.BlockSpec(memory_space=pltpu.HBM),
        ],
        out_specs=[pl.BlockSpec(memory_space=pltpu.VMEM)] * 2,
        scratch_shapes=[
            pltpu.VMEM((2, FIELDS, 256, LANES), f32),
            pltpu.VMEM((2, FIELDS, 16, LANES), f32),
            pltpu.VMEM((FIELDS, 16, LANES), f32),
            pltpu.VMEM((2, FIELDS, 3) + plane, f32),
            pltpu.VMEM((2, FIELDS, 3) + plane, f32),
            pltpu.VMEM((3, 2, FIELDS, 3) + plane, f32),
            pltpu.VMEM((3, 2, FIELDS, 3) + plane, f32),
            pltpu.VMEM((FIELDS, 16, LANES), f32),
            pltpu.VMEM((FIELDS, 16, LANES), f32),
            pltpu.VMEM((2, FIELDS) + plane, f32),
            pltpu.VMEM((FIELDS,) + plane, f32),
            pltpu.VMEM((FIELDS,) + plane, f32),
            pltpu.VMEM((2, 4, FIELDS) + plane, f32),
            pltpu.SemaphoreType.DMA((5,)),
            pltpu.SemaphoreType.DMA((16,)),
            pltpu.SemaphoreType.DMA((16,)),
        ],
        compiler_params=pltpu.CompilerParams(collective_id=0, has_side_effects=True),
    )(fine_links, fine, coarse, register)
    updated = updated.reshape(2, FIELDS, 4, 8, 8, LANES).transpose(0, 1, 2, 4, 3, 5)
    faces = faces.reshape(1, FIELDS, 8, 2, LANES).transpose(0, 3, 1, 2, 4)
    return (updated.reshape(2, FIELDS, 32, 1024), faces.reshape(1, 2, FIELDS, 1024))


def solution(mesh):
    in_specs = (
        P(("gx", "gy"), None, None, None),
        P(("gx", "gy"), None, None),
        P(("gx", "gy"), None, None, None, None),
        P(("gx", "gy"), None, None, None),
    )
    out_specs = (P(("gx", "gy"), None, None, None), P(("gx", "gy"), None, None, None))
    return jax.shard_map(shards, mesh=mesh, in_specs=in_specs, out_specs=out_specs, check_vma=False)
```

```python
import jax
import jax.numpy as jnp
from jax import lax
from jax.experimental import pallas as pl
from jax.experimental.pallas import tpu as pltpu
from jax.sharding import PartitionSpec as P

MESH = pl.DeviceIdType.MESH
FIELDS = 5
ROWS, LANES = 8, 128


def plane_rows(x):
    return pl.ds((x // 8) * 64 + x % 8, ROWS, stride=8)


def load_plane(ref, block, x):
    return [ref[block, f, plane_rows(x), :] for f in range(FIELDS)]


def primitive(cell):
    rho, mx, my, mz, energy = cell
    inverse = 1.0 / rho
    u, v, w = mx * inverse, my * inverse, mz * inverse
    p = 0.4 * (energy - 0.5 * (mx * u + my * v + mz * w))
    return [rho, u, v, w, p, inverse]


def edge(w0, w1, w2, w3):
    return [
        (7.0 / 12.0) * (w1[f] + w2[f]) - (1.0 / 12.0) * (w0[f] + w3[f]) for f in range(FIELDS)
    ]


def square_root(x):
    return jnp.sqrt(x)


def states(w, low, high):
    u = w[1]
    c = square_root(1.4 * w[4] * w[5])
    up = 0.1 * jnp.maximum(u + c, 0.0)
    down = 0.1 * jnp.maximum(c - u, 0.0)
    half_up, keep_up = 0.5 * up, 1.0 - (2.0 / 3.0) * up
    half_down, keep_down = 0.5 * down, 1.0 - (2.0 / 3.0) * down
    upper, lower = [], []
    for f in range(FIELDS):
        diff = high[f] - low[f]
        curve = 6.0 * w[f] - 3.0 * (low[f] + high[f])
        upper.append(high[f] - half_up * (diff - keep_up * curve))
        lower.append(low[f] + half_down * (diff + keep_down * curve))
    return upper, lower


def hllc(left, right):
    rho_l, u_l, v_l, w_l, p_l = left
    rho_r, u_r, v_r, w_r, p_r = right
    t_l, t_r = p_l / rho_l, p_r / rho_r
    c_l, c_r = square_root(1.4 * t_l), square_root(1.4 * t_r)
    s_l = jnp.minimum(u_l - c_l, u_r - c_r)
    s_r = jnp.maximum(u_l + c_l, u_r + c_r)
    m_l, m_r = rho_l * (s_l - u_l), rho_r * (s_r - u_r)
    contact = (p_r - p_l + m_l * u_l - m_r * u_r) / (m_l - m_r)
    is_left = jnp.maximum(s_l, contact) >= 0.0

    def pick(a, b):
        return jnp.where(is_left, a, b)

    u, v, w, p, t = (pick(a, b) for a, b in zip((u_l, v_l, w_l, p_l, t_l), (u_r, v_r, w_r, p_r, t_r)))
    m, s = pick(m_l, m_r), pick(s_l, s_r)
    star = pick(-s_l, s_r) > 0.0
    speed = jnp.where(star, contact, u)
    inverse = 1.0 / (s - speed)
    mass = m * inverse * speed
    gap = speed - u
    pressure = p + m * gap
    kinetic = 0.5 * (u * u + v * v + w * w)
    return [
        mass,
        mass * speed + pressure,
        mass * v,
        mass * w,
        mass * (2.5 * t + kinetic + gap * speed) + speed * (gap * p * inverse + pressure),
    ]


def three_fluxes(w):
    a = [edge(w[i], w[i + 1], w[i + 2], w[i + 3]) for i in range(5)]
    sides = [states(w[i + 2], a[i], a[i + 1]) for i in range(4)]
    return [hllc(sides[i][0], sides[i + 1][1]) for i in range(3)]


def iotas():
    return (
        lax.broadcasted_iota(jnp.int32, (ROWS, LANES), 0),
        lax.broadcasted_iota(jnp.int32, (ROWS, LANES), 1),
    )


def prolong(value, q):
    row, lane = iotas()
    rows = (q // 2) * 4 + row // 2
    lanes = ((row % 2) * 2 + lane // 64) * 32 + (q % 2) * 16 + (lane % 32) // 2
    return jnp.take_along_axis(jnp.take_along_axis(value, rows, axis=0), lanes, axis=1)


def patch(flux, q):
    row, lane = iotas()
    total = flux + pltpu.roll(flux, LANES - 1, 1)
    total = total + pltpu.roll(total, LANES - 32, 1)
    lanes = ((lane // 32) % 2) * 64 + 2 * (lane % 16)
    rows = 2 * (row % 4) + lane // 64
    placed = jnp.take_along_axis(jnp.take_along_axis(total, lanes, axis=1), rows, axis=0)
    inside = (row // 4 == q // 2) & ((lane % 32) // 16 == q % 2)
    return jnp.where(inside, 0.125 * placed, 0.0)


def single_flux(w):
    a = [edge(w[i], w[i + 1], w[i + 2], w[i + 3]) for i in range(3)]
    upper, _ = states(w[2], a[0], a[1])
    _, lower = states(w[3], a[1], a[2])
    return hllc(upper, lower)


def coarse_ghosts(ref, side, q):
    near, far = (
        primitive([prolong(ref[f, pl.ds(layer, ROWS, stride=2), :], q) for f in range(FIELDS)])
        for layer in range(2)
    )
    return [far, near, near] if side == 0 else [near, near, far]


def edge_planes(cells, block, side, ghosts, store):
    planes = range(5) if side == 0 else range(27, 32)
    inner = [load_plane(cells, block, x) for x in planes]
    w = [primitive(c) for c in inner]
    fluxes = three_fluxes(ghosts + w if side == 0 else w + ghosts)
    for k, i in enumerate((0, 1) if side == 0 else (3, 4)):
        for f in range(FIELDS):
            store(f, planes[i], inner[i][f] - 0.1 * (fluxes[k + 1][f] - fluxes[k][f]))
    return (fluxes[0], fluxes[2]) if side == 0 else (fluxes[2], fluxes[0])


def bulk(cells, out, kept, block):
    first = [load_plane(cells, block, x) for x in range(6)]
    w = [primitive(c) for c in first]
    a = [edge(w[i], w[i + 1], w[i + 2], w[i + 3]) for i in range(3)]
    upper2, _ = states(w[2], a[0], a[1])
    upper3, lower3 = states(w[3], a[1], a[2])
    flux3 = hllc(upper2, lower3)
    for f in range(FIELDS):
        kept[block, 0, f] = flux3[f]

    def step(i, carry):
        w0, w1, w2, low, upper, flux = carry
        w3 = primitive(load_plane(cells, block, i + 2))
        high = edge(w0, w1, w2, w3)
        next_upper, lower = states(w1, low, high)
        next_flux = hllc(upper, lower)
        here = plane_rows(i - 1)
        for f in range(FIELDS):
            out[block, f, here, :] = cells[block, f, here, :] - 0.1 * (next_flux[f] - flux[f])
        return w1, w2, w3, high, next_upper, next_flux

    carry = (w[3], w[4], w[5], a[2], upper3, flux3)
    carry = lax.fori_loop(0, 13, lambda k, c: step(5 + 2 * k, step(4 + 2 * k, c)), carry)
    for f in range(FIELDS):
        kept[block, 1, f] = carry[5][f]


def exchange(
    n_gx, n_gy, links, fine, coarse, register,
    out, cells, from_below, from_above, kept, faces_out,
    own_coarse, own_register, low_faces, high_faces, own_q,
    coarse_below, coarse_above, low_below, high_above, q_below, q_above,
    local_sem, send_sem, recv_sem,
):
    gx, gy = lax.axis_index("gx"), lax.axis_index("gy")
    above = (lax.rem(gx + 1, n_gx), gy)
    below = (lax.rem(gx + n_gx - 1, n_gx), gy)
    right = (gx, lax.rem(gy + 1, n_gy))
    left = (gx, lax.rem(gy + n_gy - 1, n_gy))

    def fetch(src, dst, k):
        copy = pltpu.make_async_copy(src, dst, local_sem.at[k])
        copy.start()
        return copy

    def rows(ref, start, size):
        return ref.at[:, :, pl.ds(start, size), :]

    high_in = fetch(rows(fine, 192, 64), rows(cells, 192, 64), 0)
    low_in = fetch(rows(fine, 0, 64), rows(cells, 0, 64), 1)
    middle_in = fetch(rows(fine, 64, 128), rows(cells, 64, 128), 2)
    coarse_in = fetch(coarse, own_coarse, 3)
    register_in = fetch(register, own_register, 4)

    barrier = pltpu.get_barrier_semaphore()
    for device in (above, below, right, left):
        pl.semaphore_signal(barrier, inc=1, device_id=device, device_id_type=MESH)
    pl.semaphore_wait(barrier, 4)

    sent = []

    def send(src, dst, device):
        k = len(sent)
        copy = pltpu.make_async_remote_copy(
            src_ref=src, dst_ref=dst, send_sem=send_sem.at[k], recv_sem=recv_sem.at[k],
            device_id=device, device_id_type=MESH,
        )
        copy.start()
        sent.append(copy)
        return copy

    coarse_up = send(coarse.at[0], coarse_below, above)
    high_in.wait()
    for b in range(2):
        for f in range(FIELDS):
            for x in range(3):
                high_faces[b, f, x] = cells[b, f, plane_rows(29 + x), :]
    fine_up = [send(high_faces.at[b], from_below.at[1, b], above) for b in range(2)]
    low_in.wait()
    for b in range(2):
        for f in range(FIELDS):
            for x in range(3):
                low_faces[b, f, x] = cells[b, f, plane_rows(x), :]
    for side in range(2):
        own_q[side] = jnp.full((ROWS, LANES), links[0, side, 4], jnp.int32)
    low_up = send(low_faces.at[0], low_below, above)
    q_up = send(own_q.at[0], q_below, above)
    coarse_down = send(coarse.at[1], coarse_above, below)
    fine_down = [send(low_faces.at[b], from_above.at[1, b], below) for b in range(2)]
    high_down = send(high_faces.at[0], high_above, below)
    q_down = send(own_q.at[1], q_above, below)

    def forward(copies, ref):
        for b in range(2):
            copies[b].wait_recv()
            forwards.append(send(ref.at[1, b], ref.at[0, b], right))
            forwards.append(send(ref.at[1, b], ref.at[2, b], left))

    forwards = []
    forward(fine_down, from_above)
    middle_in.wait()
    bulk(cells, out, kept, 0)
    forward(fine_up, from_below)
    bulk(cells, out, kept, 1)

    def store(f, x, value):
        out[0, f, plane_rows(x), :] = value

    coarse_down.wait_recv()
    coarse_up.wait_recv()
    for side in range(2):
        ghosts = coarse_ghosts(coarse_above if side == 0 else coarse_below, side, links[0, side, 4])
        _, third = edge_planes(cells, 0, side, ghosts, store)
        x = 2 if side == 0 else 29
        for f in range(FIELDS):
            change = kept[0, 0, f] - third[f] if side == 0 else third[f] - kept[0, 1, f]
            store(f, x, cells[0, f, plane_rows(x), :] - 0.1 * change)

    coarse_in.wait()
    register_in.wait()
    for copy in (high_down, q_down, low_up, q_up):
        copy.wait_recv()
    for t in range(2):
        side = 1 - t
        q = q_below[...] if side == 0 else q_above[...]
        planes = low_below if side == 0 else high_above
        ghosts = coarse_ghosts(own_coarse.at[t], side, q)
        w = [primitive([planes[f, x] for f in range(FIELDS)]) for x in range(3)]
        flux = single_flux(ghosts + w if side == 0 else w + ghosts)
        factor = 0.05 if t == 0 else -0.05
        here = pl.ds(t, ROWS, stride=2)
        for f in range(FIELDS):
            faces_out[f, here, :] = own_coarse[t, f, pl.ds(0, ROWS, stride=2), :] + factor * (
                own_register[f, here, :] + patch(flux[f], q)
            )

    for copy in forwards:
        copy.wait_recv()
    for copy in sent:
        copy.wait_send()


def finish(
    links, done, cells, from_below, from_above, kept, faces, out, faces_out, tiles, sem,
):
    def put(src, dst, k):
        copy = pltpu.make_async_copy(src, dst, sem.at[k])
        copy.start()
        return copy

    copies = [
        put(done.at[0], out.at[0], 0),
        put(done.at[1, :, pl.ds(64, 128), :], out.at[1, :, pl.ds(64, 128), :], 1),
        put(faces, faces_out, 2),
    ]
    for side in range(2):
        base = 0 if side == 0 else 24
        ref = from_below if side == 0 else from_above

        def store(f, x, value):
            tiles[side, f, pl.ds(x - base, ROWS, stride=8), :] = value

        column, slot = links[1, side, 2], links[1, side, 3]
        ghosts = [
            primitive([ref[column, slot, f, x] for f in range(FIELDS)]) for x in range(3)
        ]
        _, third = edge_planes(cells, 1, side, ghosts, store)
        for f in range(FIELDS):
            x = 2 if side == 0 else 29
            change = kept[1, 0, f] - third[f] if side == 0 else third[f] - kept[1, 1, f]
            store(f, x, cells[1, f, plane_rows(x), :] - 0.1 * change)
            for x in range(3, 8) if side == 0 else range(24, 29):
                store(f, x, done[1, f, plane_rows(x), :])
        copies.append(put(tiles.at[side], out.at[1, :, pl.ds(192 * side, 64), :], 3 + side))
    for copy in copies:
        copy.wait()


def shards(fine_state, fine_links, coarse_edges, flux_register):
    n_gx, n_gy = lax.axis_size("gx"), lax.axis_size("gy")
    f32 = jnp.float32
    fine = fine_state.reshape(2, FIELDS, 4, 8, 8, LANES).transpose(0, 1, 2, 4, 3, 5)
    fine = fine.reshape(2, FIELDS, 256, LANES)
    coarse = coarse_edges.reshape(2, FIELDS, 2, 8, LANES).transpose(0, 1, 3, 2, 4)
    coarse = coarse.reshape(2, FIELDS, 16, LANES)
    register = flux_register.reshape(2, FIELDS, 8, LANES).transpose(1, 2, 0, 3)
    register = register.reshape(FIELDS, 16, LANES)
    plane = (ROWS, LANES)
    smem = pl.BlockSpec(memory_space=pltpu.SMEM)
    hbm = pl.BlockSpec(memory_space=pltpu.HBM)
    vmem = pl.BlockSpec(memory_space=pltpu.VMEM)
    held = pl.pallas_call(
        lambda *refs: exchange(n_gx, n_gy, *refs),
        out_shape=[
            pltpu.VMEM((2, FIELDS, 256, LANES), f32),
            pltpu.VMEM((2, FIELDS, 256, LANES), f32),
            pltpu.VMEM((3, 2, FIELDS, 3) + plane, f32),
            pltpu.VMEM((3, 2, FIELDS, 3) + plane, f32),
            pltpu.VMEM((2, 2, FIELDS) + plane, f32),
            pltpu.VMEM((FIELDS, 16, LANES), f32),
        ],
        in_specs=[smem, hbm, hbm, hbm],
        out_specs=[vmem] * 6,
        scratch_shapes=[
            pltpu.VMEM((2, FIELDS, 16, LANES), f32),
            pltpu.VMEM((FIELDS, 16, LANES), f32),
            pltpu.VMEM((2, FIELDS, 3) + plane, f32),
            pltpu.VMEM((2, FIELDS, 3) + plane, f32),
            pltpu.VMEM((2,) + plane, jnp.int32),
            pltpu.VMEM((FIELDS, 16, LANES), f32),
            pltpu.VMEM((FIELDS, 16, LANES), f32),
            pltpu.VMEM((FIELDS, 3) + plane, f32),
            pltpu.VMEM((FIELDS, 3) + plane, f32),
            pltpu.VMEM(plane, jnp.int32),
            pltpu.VMEM(plane, jnp.int32),
            pltpu.SemaphoreType.DMA((5,)),
            pltpu.SemaphoreType.DMA((18,)),
            pltpu.SemaphoreType.DMA((18,)),
        ],
        compiler_params=pltpu.CompilerParams(collective_id=0, has_side_effects=True),
    )(fine_links, fine, coarse, register)
    updated, faces = pl.pallas_call(
        finish,
        out_shape=[
            jax.ShapeDtypeStruct((2, FIELDS, 256, LANES), f32),
            jax.ShapeDtypeStruct((FIELDS, 16, LANES), f32),
        ],
        in_specs=[smem] + [vmem] * 6,
        out_specs=[hbm, hbm],
        scratch_shapes=[
            pltpu.VMEM((2, FIELDS, 64, LANES), f32),
            pltpu.SemaphoreType.DMA((5,)),
        ],
    )(fine_links, *held)
    updated = updated.reshape(2, FIELDS, 4, 8, 8, LANES).transpose(0, 1, 2, 4, 3, 5)
    faces = faces.reshape(1, FIELDS, 8, 2, LANES).transpose(0, 3, 1, 2, 4)
    return (updated.reshape(2, FIELDS, 32, 1024), faces.reshape(1, 2, FIELDS, 1024))


def solution(mesh):
    in_specs = (
        P(("gx", "gy"), None, None, None),
        P(("gx", "gy"), None, None),
        P(("gx", "gy"), None, None, None, None),
        P(("gx", "gy"), None, None, None),
    )
    out_specs = (P(("gx", "gy"), None, None, None), P(("gx", "gy"), None, None, None))
    return jax.shard_map(shards, mesh=mesh, in_specs=in_specs, out_specs=out_specs, check_vma=False)
```

```python
import jax
import jax.numpy as jnp
from jax import lax
from jax.experimental import pallas as pl
from jax.experimental.pallas import tpu as pltpu
from jax.sharding import PartitionSpec as P

MESH = pl.DeviceIdType.MESH
FIELDS = 5
ROWS, LANES = 8, 128


def plane_rows(x):
    return pl.ds((x // 8) * 64 + x % 8, ROWS, stride=8)


def load_plane(ref, block, x):
    return [ref[block, f, plane_rows(x), :] for f in range(FIELDS)]


def primitive(cell):
    rho, mx, my, mz, energy = cell
    inverse = 1.0 / rho
    u, v, w = mx * inverse, my * inverse, mz * inverse
    p = 0.4 * (energy - 0.5 * (mx * u + my * v + mz * w))
    return [rho, u, v, w, p, inverse]


def edge(w0, w1, w2, w3):
    return [
        (7.0 / 12.0) * (w1[f] + w2[f]) - (1.0 / 12.0) * (w0[f] + w3[f]) for f in range(FIELDS)
    ]


def square_root(x):
    return jnp.sqrt(x)


def states(w, low, high):
    u = w[1]
    c = square_root(1.4 * w[4] * w[5])
    up = 0.1 * jnp.maximum(u + c, 0.0)
    down = 0.1 * jnp.maximum(c - u, 0.0)
    half_up, keep_up = 0.5 * up, 1.0 - (2.0 / 3.0) * up
    half_down, keep_down = 0.5 * down, 1.0 - (2.0 / 3.0) * down
    upper, lower = [], []
    for f in range(FIELDS):
        diff = high[f] - low[f]
        curve = 6.0 * w[f] - 3.0 * (low[f] + high[f])
        upper.append(high[f] - half_up * (diff - keep_up * curve))
        lower.append(low[f] + half_down * (diff + keep_down * curve))
    return upper, lower


def hllc(left, right):
    rho_l, u_l, v_l, w_l, p_l = left
    rho_r, u_r, v_r, w_r, p_r = right
    t_l, t_r = p_l / rho_l, p_r / rho_r
    c_l, c_r = square_root(1.4 * t_l), square_root(1.4 * t_r)
    s_l = jnp.minimum(u_l - c_l, u_r - c_r)
    s_r = jnp.maximum(u_l + c_l, u_r + c_r)
    m_l, m_r = rho_l * (s_l - u_l), rho_r * (s_r - u_r)
    contact = (p_r - p_l + m_l * u_l - m_r * u_r) / (m_l - m_r)
    is_left = jnp.maximum(s_l, contact) >= 0.0

    def pick(a, b):
        return jnp.where(is_left, a, b)

    u, v, w, p, t = (pick(a, b) for a, b in zip((u_l, v_l, w_l, p_l, t_l), (u_r, v_r, w_r, p_r, t_r)))
    m, s = pick(m_l, m_r), pick(s_l, s_r)
    star = pick(-s_l, s_r) > 0.0
    speed = jnp.where(star, contact, u)
    inverse = 1.0 / (s - speed)
    mass = m * inverse * speed
    gap = speed - u
    pressure = p + m * gap
    kinetic = 0.5 * (u * u + v * v + w * w)
    return [
        mass,
        mass * speed + pressure,
        mass * v,
        mass * w,
        mass * (2.5 * t + kinetic + gap * speed) + speed * (gap * p * inverse + pressure),
    ]


def three_fluxes(w):
    a = [edge(w[i], w[i + 1], w[i + 2], w[i + 3]) for i in range(5)]
    sides = [states(w[i + 2], a[i], a[i + 1]) for i in range(4)]
    return [hllc(sides[i][0], sides[i + 1][1]) for i in range(3)]


def iotas():
    return (
        lax.broadcasted_iota(jnp.int32, (ROWS, LANES), 0),
        lax.broadcasted_iota(jnp.int32, (ROWS, LANES), 1),
    )


def prolong(value, q):
    row, lane = iotas()
    rows = (q // 2) * 4 + row // 2
    lanes = ((row % 2) * 2 + lane // 64) * 32 + (q % 2) * 16 + (lane % 32) // 2
    return jnp.take_along_axis(jnp.take_along_axis(value, rows, axis=0), lanes, axis=1)


def patch(flux, q):
    row, lane = iotas()
    total = flux + pltpu.roll(flux, LANES - 1, 1)
    total = total + pltpu.roll(total, LANES - 32, 1)
    lanes = ((lane // 32) % 2) * 64 + 2 * (lane % 16)
    rows = 2 * (row % 4) + lane // 64
    placed = jnp.take_along_axis(jnp.take_along_axis(total, lanes, axis=1), rows, axis=0)
    inside = (row // 4 == q // 2) & ((lane % 32) // 16 == q % 2)
    return jnp.where(inside, 0.125 * placed, 0.0)


def single_flux(w):
    a = [edge(w[i], w[i + 1], w[i + 2], w[i + 3]) for i in range(3)]
    upper, _ = states(w[2], a[0], a[1])
    _, lower = states(w[3], a[1], a[2])
    return hllc(upper, lower)


def coarse_ghosts(ref, side, q):
    near, far = (
        primitive([prolong(ref[f, pl.ds(layer, ROWS, stride=2), :], q) for f in range(FIELDS)])
        for layer in range(2)
    )
    return [far, near, near] if side == 0 else [near, near, far]


def edge_planes(cells, block, side, ghosts, store):
    planes = range(5) if side == 0 else range(27, 32)
    inner = [load_plane(cells, block, x) for x in planes]
    w = [primitive(c) for c in inner]
    fluxes = three_fluxes(ghosts + w if side == 0 else w + ghosts)
    for k, i in enumerate((0, 1) if side == 0 else (3, 4)):
        for f in range(FIELDS):
            store(f, planes[i], inner[i][f] - 0.1 * (fluxes[k + 1][f] - fluxes[k][f]))
    return (fluxes[0], fluxes[2]) if side == 0 else (fluxes[2], fluxes[0])


def bulk(cells, out, kept, block):
    first = [load_plane(cells, block, x) for x in range(6)]
    w = [primitive(c) for c in first]
    a = [edge(w[i], w[i + 1], w[i + 2], w[i + 3]) for i in range(3)]
    upper2, _ = states(w[2], a[0], a[1])
    upper3, lower3 = states(w[3], a[1], a[2])
    flux3 = hllc(upper2, lower3)
    for f in range(FIELDS):
        kept[block, 0, f] = flux3[f]

    def step(i, carry):
        w0, w1, w2, low, upper, flux = carry
        w3 = primitive(load_plane(cells, block, i + 2))
        high = edge(w0, w1, w2, w3)
        next_upper, lower = states(w1, low, high)
        next_flux = hllc(upper, lower)
        here = plane_rows(i - 1)
        for f in range(FIELDS):
            out[block, f, here, :] = cells[block, f, here, :] - 0.1 * (next_flux[f] - flux[f])
        return w1, w2, w3, high, next_upper, next_flux

    carry = (w[3], w[4], w[5], a[2], upper3, flux3)
    carry = lax.fori_loop(0, 13, lambda k, c: step(5 + 2 * k, step(4 + 2 * k, c)), carry)
    for f in range(FIELDS):
        kept[block, 1, f] = carry[5][f]


def block_one_edge(side, ghost_planes, cells, kept, store):
    ghosts = [primitive(plane) for plane in ghost_planes]
    _, third = edge_planes(cells, 1, side, ghosts, store)
    x = 2 if side == 0 else 29
    for f in range(FIELDS):
        change = kept[1, 0, f] - third[f] if side == 0 else third[f] - kept[1, 1, f]
        store(f, x, cells[1, f, plane_rows(x), :] - 0.1 * change)


def exchange(
    n_gx, n_gy, links_in, fine, coarse, register,
    out, cells, low_ghosts, kept, faces_out,
    from_below, from_above, links, own_coarse, own_register, low_faces, high_faces, own_q,
    coarse_below, coarse_above, low_below, high_above, q_below, q_above,
    local_sem, send_sem, recv_sem, relay_sem, beside_sem,
):
    gx, gy = lax.axis_index("gx"), lax.axis_index("gy")
    above = (lax.rem(gx + 1, n_gx), gy)
    below = (lax.rem(gx + n_gx - 1, n_gx), gy)
    right = (gx, lax.rem(gy + 1, n_gy))
    left = (gx, lax.rem(gy + n_gy - 1, n_gy))
    is_first = gx == 0
    is_last = gx == n_gx - 1

    def fetch(src, dst, k):
        copy = pltpu.make_async_copy(src, dst, local_sem.at[k])
        copy.start()
        return copy

    def rows(ref, start, size):
        return ref.at[:, :, pl.ds(start, size), :]

    def signal(semaphore, device):
        pl.semaphore_signal(semaphore, inc=1, device_id=device, device_id_type=MESH)

    high_in = [
        fetch(fine.at[b, :, pl.ds(192, 64), :], cells.at[b, :, pl.ds(192, 64), :], b)
        for b in range(2)
    ]

    barrier = pltpu.get_barrier_semaphore()
    signal(barrier, below)

    @pl.when(jnp.logical_not(is_last))
    def _():
        signal(barrier, right)
        signal(barrier, left)

    low_in = fetch(rows(fine, 0, 64), rows(cells, 0, 64), 2)
    links_in_copy = fetch(links_in, links, 3)
    middle_in = fetch(rows(fine, 64, 128), rows(cells, 64, 128), 4)
    coarse_in = fetch(coarse, own_coarse, 5)
    register_in = fetch(register, own_register, 6)

    pl.semaphore_wait(barrier, jnp.where(is_last, 1, 3))

    def remote(src, dst, device, k):
        return pltpu.make_async_remote_copy(
            src_ref=src, dst_ref=dst, send_sem=send_sem.at[k], recv_sem=recv_sem.at[k],
            device_id=device, device_id_type=MESH,
        )

    coarse_up = remote(coarse.at[0], coarse_below, above, 0)
    fine_up = [remote(high_faces.at[b], from_below.at[1, b], above, 1 + b) for b in range(2)]
    low_up = remote(low_faces.at[0], low_below, above, 3)
    q_up = remote(own_q.at[0], q_below, above, 4)
    coarse_down = remote(coarse.at[1], coarse_above, below, 5)
    fine_down = [remote(low_faces.at[b], from_above.at[1, b], below, 6 + b) for b in range(2)]
    high_down = remote(high_faces.at[0], high_above, below, 8)
    q_down = remote(own_q.at[1], q_above, below, 9)
    on_up, on_down = (
        [
            [
                remote(ref.at[1, b], ref.at[0, b], right, base + 2 * b),
                remote(ref.at[1, b], ref.at[2, b], left, base + 2 * b + 1),
            ]
            for b in range(2)
        ]
        for ref, base in ((from_below, 10), (from_above, 14))
    )

    for b in range(2):
        high_in[b].wait()
        for f in range(FIELDS):
            for x in range(3):
                high_faces[b, f, x] = cells[b, f, plane_rows(29 + x), :]
        fine_up[b].start()
    low_in.wait()
    for b in range(2):
        for f in range(FIELDS):
            for x in range(3):
                low_faces[b, f, x] = cells[b, f, plane_rows(x), :]
    links_in_copy.wait()
    for side in range(2):
        own_q[side] = jnp.full((ROWS, LANES), links[0, side, 4], jnp.int32)
    middle_in.wait()
    bulk(cells, out, kept, 0)
    for copy in fine_up:
        copy.wait_send()
    coarse_up.start()
    low_up.start()
    q_up.start()
    bulk(cells, out, kept, 1)

    def forward(arriving, onward):
        for b in range(2):
            arriving[b].wait_recv()
            for copy in onward[b]:
                copy.start()

    def send_down():
        for copy in [coarse_down] + fine_down + [high_down, q_down]:
            copy.start()

    @pl.when(is_first)
    def _():
        forward(fine_down, on_down)

    fine_up[0].wait_recv()

    @pl.when(jnp.logical_not(is_first))
    def _():
        send_down()

    @pl.when(is_last)
    def _():
        pl.semaphore_wait(beside_sem, 1)

    for copy in on_up[0]:
        copy.start()
    fine_up[1].wait_recv()
    for copy in on_up[1]:
        copy.start()

    @pl.when(is_first)
    def _():
        signal(relay_sem.at[0], right)
        signal(relay_sem.at[1], left)
        send_down()
        pl.semaphore_wait(relay_sem.at[0], 1)
        pl.semaphore_wait(relay_sem.at[1], 1)
        signal(beside_sem, below)

    @pl.when(jnp.logical_not(is_first))
    def _():
        forward(fine_down, on_down)

    def store(f, x, value):
        out[0, f, plane_rows(x), :] = value

    coarse_down.wait_recv()
    coarse_up.wait_recv()
    for side in range(2):
        ghosts = coarse_ghosts(coarse_above if side == 0 else coarse_below, side, links[0, side, 4])
        _, third = edge_planes(cells, 0, side, ghosts, store)
        x = 2 if side == 0 else 29
        for f in range(FIELDS):
            change = kept[0, 0, f] - third[f] if side == 0 else third[f] - kept[0, 1, f]
            store(f, x, cells[0, f, plane_rows(x), :] - 0.1 * change)

    def store_one(f, x, value):
        out[1, f, plane_rows(x), :] = value

    for pair in on_down:
        for copy in pair:
            copy.wait_recv()
    column, slot = links[1, 1, 2], links[1, 1, 3]
    ghost_planes = [[from_above[column, slot, f, x] for f in range(FIELDS)] for x in range(3)]
    block_one_edge(1, ghost_planes, cells, kept, store_one)

    coarse_in.wait()
    register_in.wait()
    for copy in (high_down, q_down, low_up, q_up):
        copy.wait_recv()
    for t in range(2):
        side = 1 - t
        q = q_below[...] if side == 0 else q_above[...]
        planes = low_below if side == 0 else high_above
        ghosts = coarse_ghosts(own_coarse.at[t], side, q)
        w = [primitive([planes[f, x] for f in range(FIELDS)]) for x in range(3)]
        flux = single_flux(ghosts + w if side == 0 else w + ghosts)
        factor = 0.05 if t == 0 else -0.05
        here = pl.ds(t, ROWS, stride=2)
        for f in range(FIELDS):
            faces_out[f, here, :] = own_coarse[t, f, pl.ds(0, ROWS, stride=2), :] + factor * (
                own_register[f, here, :] + patch(flux[f], q)
            )

    for copy in [coarse_up, low_up, q_up, coarse_down, high_down, q_down] + fine_down:
        copy.wait_send()
    for pair in on_down + on_up:
        for copy in pair:
            copy.wait_send()

    for pair in on_up:
        for copy in pair:
            copy.wait_recv()
    column, slot = links[1, 0, 2], links[1, 0, 3]
    for f in range(FIELDS):
        for x in range(3):
            low_ghosts[f, x] = from_below[column, slot, f, x]


def finish(done, cells, low_ghosts, kept, faces, out, faces_out, tile, sem):
    def put(src, dst, k):
        copy = pltpu.make_async_copy(src, dst, sem.at[k])
        copy.start()
        return copy

    copies = [
        put(done.at[0], out.at[0], 0),
        put(done.at[1, :, pl.ds(64, 192), :], out.at[1, :, pl.ds(64, 192), :], 1),
        put(faces, faces_out, 2),
    ]

    def store(f, x, value):
        tile[f, pl.ds(x, ROWS, stride=8), :] = value

    ghost_planes = [[low_ghosts[f, x] for f in range(FIELDS)] for x in range(3)]
    block_one_edge(0, ghost_planes, cells, kept, store)
    for f in range(FIELDS):
        for x in range(3, 8):
            store(f, x, done[1, f, plane_rows(x), :])
    copies.append(put(tile, out.at[1, :, pl.ds(0, 64), :], 3))
    for copy in copies:
        copy.wait()


def shards(fine_state, fine_links, coarse_edges, flux_register):
    n_gx, n_gy = lax.axis_size("gx"), lax.axis_size("gy")
    f32 = jnp.float32
    fine = fine_state.reshape(2, FIELDS, 4, 8, 8, LANES).transpose(0, 1, 2, 4, 3, 5)
    fine = fine.reshape(2, FIELDS, 256, LANES)
    coarse = coarse_edges.reshape(2, FIELDS, 2, 8, LANES).transpose(0, 1, 3, 2, 4)
    coarse = coarse.reshape(2, FIELDS, 16, LANES)
    register = flux_register.reshape(2, FIELDS, 8, LANES).transpose(1, 2, 0, 3)
    register = register.reshape(FIELDS, 16, LANES)
    plane = (ROWS, LANES)
    hbm = pl.BlockSpec(memory_space=pltpu.HBM)
    vmem = pl.BlockSpec(memory_space=pltpu.VMEM)
    held = pl.pallas_call(
        lambda *refs: exchange(n_gx, n_gy, *refs),
        out_shape=[
            pltpu.VMEM((2, FIELDS, 256, LANES), f32),
            pltpu.VMEM((2, FIELDS, 256, LANES), f32),
            pltpu.VMEM((FIELDS, 3) + plane, f32),
            pltpu.VMEM((2, 2, FIELDS) + plane, f32),
            pltpu.VMEM((FIELDS, 16, LANES), f32),
        ],
        in_specs=[hbm] * 4,
        out_specs=[vmem] * 5,
        scratch_shapes=[
            pltpu.VMEM((3, 2, FIELDS, 3) + plane, f32),
            pltpu.VMEM((3, 2, FIELDS, 3) + plane, f32),
            pltpu.SMEM((2, 2, 5), jnp.int32),
            pltpu.VMEM((2, FIELDS, 16, LANES), f32),
            pltpu.VMEM((FIELDS, 16, LANES), f32),
            pltpu.VMEM((2, FIELDS, 3) + plane, f32),
            pltpu.VMEM((2, FIELDS, 3) + plane, f32),
            pltpu.VMEM((2,) + plane, jnp.int32),
            pltpu.VMEM((FIELDS, 16, LANES), f32),
            pltpu.VMEM((FIELDS, 16, LANES), f32),
            pltpu.VMEM((FIELDS, 3) + plane, f32),
            pltpu.VMEM((FIELDS, 3) + plane, f32),
            pltpu.VMEM(plane, jnp.int32),
            pltpu.VMEM(plane, jnp.int32),
            pltpu.SemaphoreType.DMA((7,)),
            pltpu.SemaphoreType.DMA((18,)),
            pltpu.SemaphoreType.DMA((18,)),
            pltpu.SemaphoreType.REGULAR((2,)),
            pltpu.SemaphoreType.REGULAR,
        ],
        compiler_params=pltpu.CompilerParams(collective_id=0, has_side_effects=True),
    )(fine_links, fine, coarse, register)
    updated, faces = pl.pallas_call(
        finish,
        out_shape=[
            jax.ShapeDtypeStruct((2, FIELDS, 256, LANES), f32),
            jax.ShapeDtypeStruct((FIELDS, 16, LANES), f32),
        ],
        in_specs=[vmem] * 5,
        out_specs=[hbm, hbm],
        scratch_shapes=[
            pltpu.VMEM((FIELDS, 64, LANES), f32),
            pltpu.SemaphoreType.DMA((4,)),
        ],
        compiler_params=pltpu.CompilerParams(vmem_limit_bytes=8 * 2**20),
    )(*held)
    updated = updated.reshape(2, FIELDS, 4, 8, 8, LANES).transpose(0, 1, 2, 4, 3, 5)
    faces = faces.reshape(1, FIELDS, 8, 2, LANES).transpose(0, 3, 1, 2, 4)
    return (updated.reshape(2, FIELDS, 32, 1024), faces.reshape(1, 2, FIELDS, 1024))


def solution(mesh):
    in_specs = (
        P(("gx", "gy"), None, None, None),
        P(("gx", "gy"), None, None),
        P(("gx", "gy"), None, None, None, None),
        P(("gx", "gy"), None, None, None),
    )
    out_specs = (P(("gx", "gy"), None, None, None), P(("gx", "gy"), None, None, None))
    return jax.shard_map(shards, mesh=mesh, in_specs=in_specs, out_specs=out_specs, check_vma=False)
```

```python
import jax
import jax.numpy as jnp
from jax import lax
from jax.experimental import pallas as pl
from jax.experimental.pallas import tpu as pltpu
from jax.sharding import PartitionSpec as P

MESH = pl.DeviceIdType.MESH
FIELDS = 5
ROWS, LANES = 8, 128


def plane_rows(x):
    return pl.ds((x // 8) * 64 + x % 8, ROWS, stride=8)


def load_plane(ref, block, x):
    return [ref[block, f, plane_rows(x), :] for f in range(FIELDS)]


def planes_of(ref, x):
    return [ref[f, :, x, 0, :] for f in range(FIELDS)]


def primitive(cell):
    rho, mx, my, mz, energy = cell
    inverse = 1.0 / rho
    u, v, w = mx * inverse, my * inverse, mz * inverse
    p = 0.4 * (energy - 0.5 * (mx * u + my * v + mz * w))
    return [rho, u, v, w, p, inverse]


def edge(w0, w1, w2, w3):
    return [
        (7.0 / 12.0) * (w1[f] + w2[f]) - (1.0 / 12.0) * (w0[f] + w3[f]) for f in range(FIELDS)
    ]


def square_root(x):
    return jnp.sqrt(x)


def states(w, low, high):
    u = w[1]
    c = square_root(1.4 * w[4] * w[5])
    up = 0.1 * jnp.maximum(u + c, 0.0)
    down = 0.1 * jnp.maximum(c - u, 0.0)
    half_up, keep_up = 0.5 * up, 1.0 - (2.0 / 3.0) * up
    half_down, keep_down = 0.5 * down, 1.0 - (2.0 / 3.0) * down
    upper, lower = [], []
    for f in range(FIELDS):
        diff = high[f] - low[f]
        curve = 6.0 * w[f] - 3.0 * (low[f] + high[f])
        upper.append(high[f] - half_up * (diff - keep_up * curve))
        lower.append(low[f] + half_down * (diff + keep_down * curve))
    return upper, lower


def hllc(left, right):
    rho_l, u_l, v_l, w_l, p_l = left
    rho_r, u_r, v_r, w_r, p_r = right
    t_l, t_r = p_l / rho_l, p_r / rho_r
    c_l, c_r = square_root(1.4 * t_l), square_root(1.4 * t_r)
    s_l = jnp.minimum(u_l - c_l, u_r - c_r)
    s_r = jnp.maximum(u_l + c_l, u_r + c_r)
    m_l, m_r = rho_l * (s_l - u_l), rho_r * (s_r - u_r)
    contact = (p_r - p_l + m_l * u_l - m_r * u_r) / (m_l - m_r)
    is_left = jnp.maximum(s_l, contact) >= 0.0

    def pick(a, b):
        return jnp.where(is_left, a, b)

    u, v, w, p, t = (pick(a, b) for a, b in zip((u_l, v_l, w_l, p_l, t_l), (u_r, v_r, w_r, p_r, t_r)))
    m, s = pick(m_l, m_r), pick(s_l, s_r)
    star = pick(-s_l, s_r) > 0.0
    speed = jnp.where(star, contact, u)
    inverse = 1.0 / (s - speed)
    mass = m * inverse * speed
    gap = speed - u
    pressure = p + m * gap
    kinetic = 0.5 * (u * u + v * v + w * w)
    return [
        mass,
        mass * speed + pressure,
        mass * v,
        mass * w,
        mass * (2.5 * t + kinetic + gap * speed) + speed * (gap * p * inverse + pressure),
    ]


def three_fluxes(w):
    a = [edge(w[i], w[i + 1], w[i + 2], w[i + 3]) for i in range(5)]
    sides = [states(w[i + 2], a[i], a[i + 1]) for i in range(4)]
    return [hllc(sides[i][0], sides[i + 1][1]) for i in range(3)]


def iotas():
    return (
        lax.broadcasted_iota(jnp.int32, (ROWS, LANES), 0),
        lax.broadcasted_iota(jnp.int32, (ROWS, LANES), 1),
    )


def prolong(value, q):
    row, lane = iotas()
    rows = (q // 2) * 4 + row // 2
    lanes = ((row % 2) * 2 + lane // 64) * 32 + (q % 2) * 16 + (lane % 32) // 2
    return jnp.take_along_axis(jnp.take_along_axis(value, rows, axis=0), lanes, axis=1)


def patch(flux, q):
    row, lane = iotas()
    total = flux + pltpu.roll(flux, LANES - 1, 1)
    total = total + pltpu.roll(total, LANES - 32, 1)
    lanes = ((lane // 32) % 2) * 64 + 2 * (lane % 16)
    rows = 2 * (row % 4) + lane // 64
    placed = jnp.take_along_axis(jnp.take_along_axis(total, lanes, axis=1), rows, axis=0)
    inside = (row // 4 == q // 2) & ((lane % 32) // 16 == q % 2)
    return jnp.where(inside, 0.125 * placed, 0.0)


def single_flux(w):
    a = [edge(w[i], w[i + 1], w[i + 2], w[i + 3]) for i in range(3)]
    upper, _ = states(w[2], a[0], a[1])
    _, lower = states(w[3], a[1], a[2])
    return hllc(upper, lower)


def coarse_ghosts(ref, side, q):
    near, far = (
        primitive([prolong(ref[f, pl.ds(layer, ROWS, stride=2), :], q) for f in range(FIELDS)])
        for layer in range(2)
    )
    return [far, near, near] if side == 0 else [near, near, far]


def edge_planes(cells, block, side, ghosts, store):
    planes = range(5) if side == 0 else range(27, 32)
    inner = [load_plane(cells, block, x) for x in planes]
    w = [primitive(c) for c in inner]
    fluxes = three_fluxes(ghosts + w if side == 0 else w + ghosts)
    for k, i in enumerate((0, 1) if side == 0 else (3, 4)):
        for f in range(FIELDS):
            store(f, planes[i], inner[i][f] - 0.1 * (fluxes[k + 1][f] - fluxes[k][f]))
    return (fluxes[0], fluxes[2]) if side == 0 else (fluxes[2], fluxes[0])


def bulk(cells, out, kept, block):
    first = [load_plane(cells, block, x) for x in range(6)]
    w = [primitive(c) for c in first]
    a = [edge(w[i], w[i + 1], w[i + 2], w[i + 3]) for i in range(3)]
    upper2, _ = states(w[2], a[0], a[1])
    upper3, lower3 = states(w[3], a[1], a[2])
    flux3 = hllc(upper2, lower3)
    for f in range(FIELDS):
        kept[block, 0, f] = flux3[f]

    def step(i, carry):
        w0, w1, w2, low, upper, flux = carry
        w3 = primitive(load_plane(cells, block, i + 2))
        high = edge(w0, w1, w2, w3)
        next_upper, lower = states(w1, low, high)
        next_flux = hllc(upper, lower)
        here = plane_rows(i - 1)
        for f in range(FIELDS):
            out[block, f, here, :] = cells[block, f, here, :] - 0.1 * (next_flux[f] - flux[f])
        return w1, w2, w3, high, next_upper, next_flux

    carry = (w[3], w[4], w[5], a[2], upper3, flux3)
    carry = lax.fori_loop(0, 13, lambda k, c: step(5 + 2 * k, step(4 + 2 * k, c)), carry)
    for f in range(FIELDS):
        kept[block, 1, f] = carry[5][f]


def block_one_edge(side, ghost_planes, cells, kept, store):
    ghosts = [primitive(plane) for plane in ghost_planes]
    _, third = edge_planes(cells, 1, side, ghosts, store)
    x = 2 if side == 0 else 29
    for f in range(FIELDS):
        change = kept[1, 0, f] - third[f] if side == 0 else third[f] - kept[1, 1, f]
        store(f, x, cells[1, f, plane_rows(x), :] - 0.1 * change)


def exchange(
    n_gx, n_gy, links_in, fine, planes, coarse, register,
    out, cells, low_ghosts, kept, faces_out,
    from_below, from_above, links, own_coarse, own_register,
    coarse_below, coarse_above, low_below, high_above, links_below, links_above,
    local_sem, send_sem, recv_sem, relay_sem, beside_sem, below_sem,
):
    gx, gy = lax.axis_index("gx"), lax.axis_index("gy")
    above = (lax.rem(gx + 1, n_gx), gy)
    below = (lax.rem(gx + n_gx - 1, n_gx), gy)
    right = (gx, lax.rem(gy + 1, n_gy))
    left = (gx, lax.rem(gy + n_gy - 1, n_gy))
    is_first = gx == 0
    is_last = gx == n_gx - 1

    def fetch(src, dst, k):
        copy = pltpu.make_async_copy(src, dst, local_sem.at[k])
        copy.start()
        return copy

    def signal(semaphore, device):
        pl.semaphore_signal(semaphore, inc=1, device_id=device, device_id_type=MESH)

    barrier = pltpu.get_barrier_semaphore()
    signal(barrier, below)

    @pl.when(jnp.logical_not(is_last))
    def _():
        signal(barrier, right)
        signal(barrier, left)

    pl.semaphore_wait(barrier, jnp.where(is_last, 1, 3))
    signal(below_sem, above)

    def remote(src, dst, device, k):
        return pltpu.make_async_remote_copy(
            src_ref=src, dst_ref=dst, send_sem=send_sem.at[k], recv_sem=recv_sem.at[k],
            device_id=device, device_id_type=MESH,
        )

    def high(b):
        return planes.at[b, :, 3, :, pl.ds(5, 3)]

    def low(b):
        return planes.at[b, :, 0, :, pl.ds(0, 3)]

    fine_up = [remote(high(b), from_below.at[1, b], above, b) for b in range(2)]
    coarse_up = remote(coarse.at[0], coarse_below, above, 2)
    low_up = remote(low(0), low_below, above, 3)
    links_up = remote(links_in, links_below, above, 4)
    coarse_down = remote(coarse.at[1], coarse_above, below, 5)
    fine_down = [remote(low(b), from_above.at[1, b], below, 6 + b) for b in range(2)]
    high_down = remote(high(0), high_above, below, 8)
    links_down = remote(links_in, links_above, below, 9)
    on_up, on_down = (
        [
            [
                remote(ref.at[1, b], ref.at[0, b], right, base + 2 * b),
                remote(ref.at[1, b], ref.at[2, b], left, base + 2 * b + 1),
            ]
            for b in range(2)
        ]
        for ref, base in ((from_below, 10), (from_above, 14))
    )

    for copy in fine_up:
        copy.start()
    cells_in = [fetch(fine.at[b], cells.at[b], b) for b in range(2)]
    links_copy = fetch(links_in, links, 2)
    coarse_in = fetch(coarse, own_coarse, 3)
    register_in = fetch(register, own_register, 4)
    cells_in[0].wait()
    bulk(cells, out, kept, 0)
    for copy in fine_up:
        copy.wait_send()
    coarse_up.start()
    low_up.start()
    links_up.start()
    cells_in[1].wait()
    bulk(cells, out, kept, 1)

    def forward(arriving, onward):
        for b in range(2):
            arriving[b].wait_recv()
            for copy in onward[b]:
                copy.start()

    def send_down():
        for copy in [coarse_down] + fine_down + [high_down, links_down]:
            copy.start()

    @pl.when(is_first)
    def _():
        forward(fine_down, on_down)

    pl.semaphore_wait(below_sem, 1)
    send_down()

    @pl.when(is_first)
    def _():
        signal(relay_sem.at[0], right)
        signal(relay_sem.at[1], left)

    @pl.when(is_last)
    def _():
        pl.semaphore_wait(beside_sem, 1)

    forward(fine_up, on_up)

    @pl.when(is_first)
    def _():
        pl.semaphore_wait(relay_sem.at[0], 1)
        pl.semaphore_wait(relay_sem.at[1], 1)
        signal(beside_sem, below)

    @pl.when(jnp.logical_not(is_first))
    def _():
        forward(fine_down, on_down)

    def store(f, x, value):
        out[0, f, plane_rows(x), :] = value

    links_copy.wait()
    coarse_down.wait_recv()
    coarse_up.wait_recv()
    for side in range(2):
        ghosts = coarse_ghosts(coarse_above if side == 0 else coarse_below, side, links[0, side, 4])
        _, third = edge_planes(cells, 0, side, ghosts, store)
        x = 2 if side == 0 else 29
        for f in range(FIELDS):
            change = kept[0, 0, f] - third[f] if side == 0 else third[f] - kept[0, 1, f]
            store(f, x, cells[0, f, plane_rows(x), :] - 0.1 * change)

    def store_one(f, x, value):
        out[1, f, plane_rows(x), :] = value

    for pair in on_down:
        for copy in pair:
            copy.wait_recv()
    column, slot = links[1, 1, 2], links[1, 1, 3]
    ghost_planes = [planes_of(from_above.at[column, slot], x) for x in range(3)]
    block_one_edge(1, ghost_planes, cells, kept, store_one)

    coarse_in.wait()
    register_in.wait()
    for copy in (high_down, links_down, low_up, links_up):
        copy.wait_recv()
    for t in range(2):
        side = 1 - t
        their_links = links_below if side == 0 else links_above
        q = jnp.broadcast_to(their_links[0][side : side + 1, 4:5], (ROWS, LANES))
        outer = low_below if side == 0 else high_above
        ghosts = coarse_ghosts(own_coarse.at[t], side, q)
        w = [primitive(planes_of(outer, x)) for x in range(3)]
        flux = single_flux(ghosts + w if side == 0 else w + ghosts)
        factor = 0.05 if t == 0 else -0.05
        here = pl.ds(t, ROWS, stride=2)
        for f in range(FIELDS):
            faces_out[f, here, :] = own_coarse[t, f, pl.ds(0, ROWS, stride=2), :] + factor * (
                own_register[f, here, :] + patch(flux[f], q)
            )

    for copy in [coarse_up, low_up, links_up, coarse_down, high_down, links_down] + fine_down:
        copy.wait_send()
    for pair in on_down + on_up:
        for copy in pair:
            copy.wait_send()

    for pair in on_up:
        for copy in pair:
            copy.wait_recv()
    column, slot = links[1, 0, 2], links[1, 0, 3]
    for x in range(3):
        for f, value in enumerate(planes_of(from_below.at[column, slot], x)):
            low_ghosts[f, x] = value


def finish(done, cells, low_ghosts, kept, faces, out, faces_out, tile, sem):
    def put(src, dst, k):
        copy = pltpu.make_async_copy(src, dst, sem.at[k])
        copy.start()
        return copy

    copies = [
        put(done.at[0], out.at[0], 0),
        put(done.at[1, :, pl.ds(64, 192), :], out.at[1, :, pl.ds(64, 192), :], 1),
        put(faces, faces_out, 2),
    ]

    def store(f, x, value):
        tile[f, pl.ds(x, ROWS, stride=8), :] = value

    ghost_planes = [[low_ghosts[f, x] for f in range(FIELDS)] for x in range(3)]
    block_one_edge(0, ghost_planes, cells, kept, store)
    for f in range(FIELDS):
        for x in range(3, 8):
            store(f, x, done[1, f, plane_rows(x), :])
    copies.append(put(tile, out.at[1, :, pl.ds(0, 64), :], 3))
    for copy in copies:
        copy.wait()


def shards(fine_state, fine_links, coarse_edges, flux_register):
    n_gx, n_gy = lax.axis_size("gx"), lax.axis_size("gy")
    f32 = jnp.float32
    fine = fine_state.reshape(2, FIELDS, 4, 8, 8, LANES).transpose(0, 1, 2, 4, 3, 5)
    planes = fine.reshape(2, FIELDS, 4, 8, 8, 1, LANES)
    fine = fine.reshape(2, FIELDS, 256, LANES)
    coarse = coarse_edges.reshape(2, FIELDS, 2, 8, LANES).transpose(0, 1, 3, 2, 4)
    coarse = coarse.reshape(2, FIELDS, 16, LANES)
    register = flux_register.reshape(2, FIELDS, 8, LANES).transpose(1, 2, 0, 3)
    register = register.reshape(FIELDS, 16, LANES)
    plane = (ROWS, LANES)
    outer = (FIELDS, ROWS, 3, 1, LANES)
    hbm = pl.BlockSpec(memory_space=pltpu.HBM)
    vmem = pl.BlockSpec(memory_space=pltpu.VMEM)
    held = pl.pallas_call(
        lambda *refs: exchange(n_gx, n_gy, *refs),
        out_shape=[
            pltpu.VMEM((2, FIELDS, 256, LANES), f32),
            pltpu.VMEM((2, FIELDS, 256, LANES), f32),
            pltpu.VMEM((FIELDS, 3) + plane, f32),
            pltpu.VMEM((2, 2, FIELDS) + plane, f32),
            pltpu.VMEM((FIELDS, 16, LANES), f32),
        ],
        in_specs=[hbm] * 5,
        out_specs=[vmem] * 5,
        scratch_shapes=[
            pltpu.VMEM((3, 2) + outer, f32),
            pltpu.VMEM((3, 2) + outer, f32),
            pltpu.SMEM((2, 2, 5), jnp.int32),
            pltpu.VMEM((2, FIELDS, 16, LANES), f32),
            pltpu.VMEM((FIELDS, 16, LANES), f32),
            pltpu.VMEM((FIELDS, 16, LANES), f32),
            pltpu.VMEM((FIELDS, 16, LANES), f32),
            pltpu.VMEM(outer, f32),
            pltpu.VMEM(outer, f32),
            pltpu.VMEM((2, 2, 5), jnp.int32),
            pltpu.VMEM((2, 2, 5), jnp.int32),
            pltpu.SemaphoreType.DMA((5,)),
            pltpu.SemaphoreType.DMA((18,)),
            pltpu.SemaphoreType.DMA((18,)),
            pltpu.SemaphoreType.REGULAR((2,)),
            pltpu.SemaphoreType.REGULAR,
            pltpu.SemaphoreType.REGULAR,
        ],
        compiler_params=pltpu.CompilerParams(collective_id=0, has_side_effects=True),
    )(fine_links, fine, planes, coarse, register)
    updated, faces = pl.pallas_call(
        finish,
        out_shape=[
            jax.ShapeDtypeStruct((2, FIELDS, 256, LANES), f32),
            jax.ShapeDtypeStruct((FIELDS, 16, LANES), f32),
        ],
        in_specs=[vmem] * 5,
        out_specs=[hbm, hbm],
        scratch_shapes=[
            pltpu.VMEM((FIELDS, 64, LANES), f32),
            pltpu.SemaphoreType.DMA((4,)),
        ],
        compiler_params=pltpu.CompilerParams(vmem_limit_bytes=8 * 2**20),
    )(*held)
    updated = updated.reshape(2, FIELDS, 4, 8, 8, LANES).transpose(0, 1, 2, 4, 3, 5)
    faces = faces.reshape(1, FIELDS, 8, 2, LANES).transpose(0, 3, 1, 2, 4)
    return (updated.reshape(2, FIELDS, 32, 1024), faces.reshape(1, 2, FIELDS, 1024))


def solution(mesh):
    in_specs = (
        P(("gx", "gy"), None, None, None),
        P(("gx", "gy"), None, None),
        P(("gx", "gy"), None, None, None, None),
        P(("gx", "gy"), None, None, None),
    )
    out_specs = (P(("gx", "gy"), None, None, None), P(("gx", "gy"), None, None, None))
    return jax.shard_map(shards, mesh=mesh, in_specs=in_specs, out_specs=out_specs, check_vma=False)
```

```python
import jax
import jax.numpy as jnp
from jax import lax
from jax.experimental import pallas as pl
from jax.experimental.pallas import tpu as pltpu
from jax.sharding import PartitionSpec as P

MESH = pl.DeviceIdType.MESH
FIELDS = 5
ROWS, LANES = 8, 128


def plane_rows(x):
    return pl.ds((x // 8) * 64 + x % 8, ROWS, stride=8)


def load_plane(ref, block, x):
    return [ref[block, f, plane_rows(x), :] for f in range(FIELDS)]


def planes_of(ref, x):
    return [ref[f, :, x, 0, :] for f in range(FIELDS)]


def primitive(cell):
    rho, mx, my, mz, energy = cell
    inverse = 1.0 / rho
    u, v, w = mx * inverse, my * inverse, mz * inverse
    p = 0.4 * (energy - 0.5 * (mx * u + my * v + mz * w))
    return [rho, u, v, w, p, inverse]


def edge(w0, w1, w2, w3):
    return [
        (7.0 / 12.0) * (w1[f] + w2[f]) - (1.0 / 12.0) * (w0[f] + w3[f]) for f in range(FIELDS)
    ]


def square_root(x):
    return jnp.sqrt(x)


def states(w, low, high):
    u = w[1]
    c = square_root(1.4 * w[4] * w[5])
    up = 0.1 * jnp.maximum(u + c, 0.0)
    down = 0.1 * jnp.maximum(c - u, 0.0)
    half_up, keep_up = 0.5 * up, 1.0 - (2.0 / 3.0) * up
    half_down, keep_down = 0.5 * down, 1.0 - (2.0 / 3.0) * down
    upper, lower = [], []
    for f in range(FIELDS):
        diff = high[f] - low[f]
        curve = 6.0 * w[f] - 3.0 * (low[f] + high[f])
        upper.append(high[f] - half_up * (diff - keep_up * curve))
        lower.append(low[f] + half_down * (diff + keep_down * curve))
    return upper, lower


def hllc(left, right):
    rho_l, u_l, v_l, w_l, p_l = left
    rho_r, u_r, v_r, w_r, p_r = right
    t_l, t_r = p_l / rho_l, p_r / rho_r
    c_l, c_r = square_root(1.4 * t_l), square_root(1.4 * t_r)
    s_l = jnp.minimum(u_l - c_l, u_r - c_r)
    s_r = jnp.maximum(u_l + c_l, u_r + c_r)
    m_l, m_r = rho_l * (s_l - u_l), rho_r * (s_r - u_r)
    contact = (p_r - p_l + m_l * u_l - m_r * u_r) / (m_l - m_r)
    is_left = jnp.maximum(s_l, contact) >= 0.0

    def pick(a, b):
        return jnp.where(is_left, a, b)

    u, v, w, p, t = (pick(a, b) for a, b in zip((u_l, v_l, w_l, p_l, t_l), (u_r, v_r, w_r, p_r, t_r)))
    m, s = pick(m_l, m_r), pick(s_l, s_r)
    star = pick(-s_l, s_r) > 0.0
    speed = jnp.where(star, contact, u)
    inverse = 1.0 / (s - speed)
    mass = m * inverse * speed
    gap = speed - u
    pressure = p + m * gap
    kinetic = 0.5 * (u * u + v * v + w * w)
    return [
        mass,
        mass * speed + pressure,
        mass * v,
        mass * w,
        mass * (2.5 * t + kinetic + gap * speed) + speed * (gap * p * inverse + pressure),
    ]


def three_fluxes(w):
    a = [edge(w[i], w[i + 1], w[i + 2], w[i + 3]) for i in range(5)]
    sides = [states(w[i + 2], a[i], a[i + 1]) for i in range(4)]
    return [hllc(sides[i][0], sides[i + 1][1]) for i in range(3)]


def iotas():
    return (
        lax.broadcasted_iota(jnp.int32, (ROWS, LANES), 0),
        lax.broadcasted_iota(jnp.int32, (ROWS, LANES), 1),
    )


def prolong(value, q):
    row, lane = iotas()
    rows = (q // 2) * 4 + row // 2
    lanes = ((row % 2) * 2 + lane // 64) * 32 + (q % 2) * 16 + (lane % 32) // 2
    return jnp.take_along_axis(jnp.take_along_axis(value, rows, axis=0), lanes, axis=1)


def patch(flux, q):
    row, lane = iotas()
    total = flux + pltpu.roll(flux, LANES - 1, 1)
    total = total + pltpu.roll(total, LANES - 32, 1)
    lanes = ((lane // 32) % 2) * 64 + 2 * (lane % 16)
    rows = 2 * (row % 4) + lane // 64
    placed = jnp.take_along_axis(jnp.take_along_axis(total, lanes, axis=1), rows, axis=0)
    inside = (row // 4 == q // 2) & ((lane % 32) // 16 == q % 2)
    return jnp.where(inside, 0.125 * placed, 0.0)


def single_flux(w):
    a = [edge(w[i], w[i + 1], w[i + 2], w[i + 3]) for i in range(3)]
    upper, _ = states(w[2], a[0], a[1])
    _, lower = states(w[3], a[1], a[2])
    return hllc(upper, lower)


def coarse_ghosts(ref, side, q):
    near, far = (
        primitive([prolong(ref[f, pl.ds(layer, ROWS, stride=2), :], q) for f in range(FIELDS)])
        for layer in range(2)
    )
    return [far, near, near] if side == 0 else [near, near, far]


def edge_planes(cells, block, side, ghosts, store):
    planes = range(5) if side == 0 else range(27, 32)
    inner = [load_plane(cells, block, x) for x in planes]
    w = [primitive(c) for c in inner]
    fluxes = three_fluxes(ghosts + w if side == 0 else w + ghosts)
    for k, i in enumerate((0, 1) if side == 0 else (3, 4)):
        for f in range(FIELDS):
            store(f, planes[i], inner[i][f] - 0.1 * (fluxes[k + 1][f] - fluxes[k][f]))
    return (fluxes[0], fluxes[2]) if side == 0 else (fluxes[2], fluxes[0])


def bulk(cells, out, kept, block):
    first = [load_plane(cells, block, x) for x in range(6)]
    w = [primitive(c) for c in first]
    a = [edge(w[i], w[i + 1], w[i + 2], w[i + 3]) for i in range(3)]
    upper2, _ = states(w[2], a[0], a[1])
    upper3, lower3 = states(w[3], a[1], a[2])
    flux3 = hllc(upper2, lower3)
    for f in range(FIELDS):
        kept[block, 0, f] = flux3[f]

    def step(i, carry):
        w0, w1, w2, low, upper, flux = carry
        w3 = primitive(load_plane(cells, block, i + 2))
        high = edge(w0, w1, w2, w3)
        next_upper, lower = states(w1, low, high)
        next_flux = hllc(upper, lower)
        here = plane_rows(i - 1)
        for f in range(FIELDS):
            out[block, f, here, :] = cells[block, f, here, :] - 0.1 * (next_flux[f] - flux[f])
        return w1, w2, w3, high, next_upper, next_flux

    carry = (w[3], w[4], w[5], a[2], upper3, flux3)
    carry = lax.fori_loop(0, 13, lambda k, c: step(5 + 2 * k, step(4 + 2 * k, c)), carry)
    for f in range(FIELDS):
        kept[block, 1, f] = carry[5][f]


def block_one_edge(side, ghost_planes, cells, kept, store):
    ghosts = [primitive(plane) for plane in ghost_planes]
    _, third = edge_planes(cells, 1, side, ghosts, store)
    x = 2 if side == 0 else 29
    for f in range(FIELDS):
        change = kept[1, 0, f] - third[f] if side == 0 else third[f] - kept[1, 1, f]
        store(f, x, cells[1, f, plane_rows(x), :] - 0.1 * change)


def exchange(
    n_gx, n_gy, links_in, fine, planes, coarse, register,
    out, cells, low_ghosts, kept, faces_out,
    from_below, from_above, links, own_coarse, own_register,
    coarse_below, coarse_above, low_below, high_above, links_below, links_above,
    local_sem, send_sem, recv_sem, relay_sem, beside_sem, below_sem,
):
    gx, gy = lax.axis_index("gx"), lax.axis_index("gy")
    above = (lax.rem(gx + 1, n_gx), gy)
    below = (lax.rem(gx + n_gx - 1, n_gx), gy)
    right = (gx, lax.rem(gy + 1, n_gy))
    left = (gx, lax.rem(gy + n_gy - 1, n_gy))
    odd = lax.rem(gy, 2) == 1
    is_first = gx == 0
    is_last = gx == n_gx - 1

    def fetch(src, dst, k):
        copy = pltpu.make_async_copy(src, dst, local_sem.at[k])
        copy.start()
        return copy

    def signal(semaphore, device):
        pl.semaphore_signal(semaphore, inc=1, device_id=device, device_id_type=MESH)

    barrier = pltpu.get_barrier_semaphore()
    signal(barrier, below)

    @pl.when(odd)
    def _():
        signal(barrier, (below[0], right[1]))

    @pl.when(jnp.logical_not(is_last))
    def _():
        signal(barrier, right)
        signal(barrier, left)

    pl.semaphore_wait(barrier, jnp.where(is_last, 1, 3) + jnp.where(odd, 0, 1))
    signal(below_sem, above)

    def remote(src, dst, device, k):
        return pltpu.make_async_remote_copy(
            src_ref=src, dst_ref=dst, send_sem=send_sem.at[k], recv_sem=recv_sem.at[k],
            device_id=device, device_id_type=MESH,
        )

    def high(b):
        return planes.at[b, :, 3, :, pl.ds(5, 3)]

    def low(b):
        return planes.at[b, :, 0, :, pl.ds(0, 3)]

    fine_up = [remote(high(b), from_below.at[1, b], above, b) for b in range(2)]
    coarse_up = remote(coarse.at[0], coarse_below, above, 2)
    low_up = remote(low(0), low_below, above, 3)
    links_up = remote(links_in, links_below, above, 4)
    coarse_down = remote(coarse.at[1], coarse_above, below, 5)
    fine_down = remote(planes.at[:, :, 0, :, pl.ds(0, 3)], from_above.at[1], below, 6)
    high_down = remote(high(0), high_above, below, 7)
    links_down = remote(links_in, links_above, below, 8)
    across_up = remote(high(1), from_below.at[2, 1], (above[0], left[1]), 12)
    on_up = [
        [
            remote(from_below.at[1, b], from_below.at[0, b], right, 9 + 2 * b),
            remote(from_below.at[1, b], from_below.at[2, b], left, 10 + 2 * b),
        ]
        for b in range(2)
    ]
    on_down = [
        remote(from_above.at[1], from_above.at[0], right, 13),
        remote(from_above.at[1], from_above.at[2], left, 14),
    ]

    fine_up[0].start()
    fine_up[1].start()

    @pl.when(jnp.logical_not(odd))
    def _():
        across_up.start()

    cells_in = [fetch(fine.at[b], cells.at[b], b) for b in range(2)]
    links_copy = fetch(links_in, links, 2)
    coarse_in = fetch(coarse, own_coarse, 3)
    register_in = fetch(register, own_register, 4)
    cells_in[0].wait()
    bulk(cells, out, kept, 0)
    for copy in fine_up:
        copy.wait_send()
    coarse_up.start()
    low_up.start()
    links_up.start()
    cells_in[1].wait()
    bulk(cells, out, kept, 1)

    def forward_down():
        fine_down.wait_recv()
        for copy in on_down:
            copy.start()

    def send_down():
        for copy in (coarse_down, fine_down, high_down, links_down):
            copy.start()

    @pl.when(is_first)
    def _():
        forward_down()

    pl.semaphore_wait(below_sem, 1)
    send_down()

    @pl.when(is_first)
    def _():
        signal(relay_sem.at[0], right)
        signal(relay_sem.at[1], left)

    @pl.when(is_last)
    def _():
        pl.semaphore_wait(beside_sem, 1)

    fine_up[0].wait_recv()
    for copy in on_up[0]:
        copy.start()
    fine_up[1].wait_recv()
    on_up[1][0].start()

    @pl.when(odd)
    def _():
        on_up[1][1].start()


    @pl.when(is_first)
    def _():
        pl.semaphore_wait(relay_sem.at[0], 1)
        pl.semaphore_wait(relay_sem.at[1], 1)
        signal(beside_sem, below)

    @pl.when(jnp.logical_not(is_first))
    def _():
        forward_down()

    def store(f, x, value):
        out[0, f, plane_rows(x), :] = value

    def block_zero_edge(side):
        ghosts = coarse_ghosts(coarse_above if side == 0 else coarse_below, side, links[0, side, 4])
        _, third = edge_planes(cells, 0, side, ghosts, store)
        x = 2 if side == 0 else 29
        for f in range(FIELDS):
            change = kept[0, 0, f] - third[f] if side == 0 else third[f] - kept[0, 1, f]
            store(f, x, cells[0, f, plane_rows(x), :] - 0.1 * change)

    def coarse_face(t):
        side = 1 - t
        their_links = links_below if side == 0 else links_above
        q = jnp.broadcast_to(their_links[0][side : side + 1, 4:5], (ROWS, LANES))
        outer = low_below if side == 0 else high_above
        ghosts = coarse_ghosts(own_coarse.at[t], side, q)
        w = [primitive(planes_of(outer, x)) for x in range(3)]
        flux = single_flux(ghosts + w if side == 0 else w + ghosts)
        factor = 0.05 if t == 0 else -0.05
        here = pl.ds(t, ROWS, stride=2)
        for f in range(FIELDS):
            faces_out[f, here, :] = own_coarse[t, f, pl.ds(0, ROWS, stride=2), :] + factor * (
                own_register[f, here, :] + patch(flux[f], q)
            )

    def store_one(f, x, value):
        out[1, f, plane_rows(x), :] = value

    links_copy.wait()
    coarse_in.wait()
    register_in.wait()
    coarse_down.wait_recv()
    block_zero_edge(0)
    for copy in (high_down, links_down):
        copy.wait_recv()
    coarse_face(0)
    for copy in on_down:
        copy.wait_recv()
    column, slot = links[1, 1, 2], links[1, 1, 3]
    ghost_planes = [planes_of(from_above.at[column, slot], x) for x in range(3)]
    block_one_edge(1, ghost_planes, cells, kept, store_one)
    coarse_up.wait_recv()
    block_zero_edge(1)
    for copy in (low_up, links_up):
        copy.wait_recv()
    coarse_face(1)

    for copy in (coarse_up, low_up, links_up, coarse_down, fine_down, high_down, links_down):
        copy.wait_send()
    for copy in on_down + on_up[0] + on_up[1]:
        copy.wait_send()

    for copy in on_up[0] + on_up[1]:
        copy.wait_recv()
    column, slot = links[1, 0, 2], links[1, 0, 3]
    for x in range(3):
        for f, value in enumerate(planes_of(from_below.at[column, slot], x)):
            low_ghosts[f, x] = value


def finish(done, cells, low_ghosts, kept, faces, out, faces_out, tile, sem):
    def put(src, dst, k):
        copy = pltpu.make_async_copy(src, dst, sem.at[k])
        copy.start()
        return copy

    copies = [
        put(done.at[0], out.at[0], 0),
        put(done.at[1, :, pl.ds(64, 192), :], out.at[1, :, pl.ds(64, 192), :], 1),
        put(faces, faces_out, 2),
    ]

    def store(f, x, value):
        tile[f, pl.ds(x, ROWS, stride=8), :] = value

    ghost_planes = [[low_ghosts[f, x] for f in range(FIELDS)] for x in range(3)]
    block_one_edge(0, ghost_planes, cells, kept, store)
    for f in range(FIELDS):
        for x in range(3, 8):
            store(f, x, done[1, f, plane_rows(x), :])
    copies.append(put(tile, out.at[1, :, pl.ds(0, 64), :], 3))
    for copy in copies:
        copy.wait()


def shards(fine_state, fine_links, coarse_edges, flux_register):
    n_gx, n_gy = lax.axis_size("gx"), lax.axis_size("gy")
    f32 = jnp.float32
    fine = fine_state.reshape(2, FIELDS, 4, 8, 8, LANES).transpose(0, 1, 2, 4, 3, 5)
    planes = fine.reshape(2, FIELDS, 4, 8, 8, 1, LANES)
    fine = fine.reshape(2, FIELDS, 256, LANES)
    coarse = coarse_edges.reshape(2, FIELDS, 2, 8, LANES).transpose(0, 1, 3, 2, 4)
    coarse = coarse.reshape(2, FIELDS, 16, LANES)
    register = flux_register.reshape(2, FIELDS, 8, LANES).transpose(1, 2, 0, 3)
    register = register.reshape(FIELDS, 16, LANES)
    plane = (ROWS, LANES)
    outer = (FIELDS, ROWS, 3, 1, LANES)
    hbm = pl.BlockSpec(memory_space=pltpu.HBM)
    vmem = pl.BlockSpec(memory_space=pltpu.VMEM)
    held = pl.pallas_call(
        lambda *refs: exchange(n_gx, n_gy, *refs),
        out_shape=[
            pltpu.VMEM((2, FIELDS, 256, LANES), f32),
            pltpu.VMEM((2, FIELDS, 256, LANES), f32),
            pltpu.VMEM((FIELDS, 3) + plane, f32),
            pltpu.VMEM((2, 2, FIELDS) + plane, f32),
            pltpu.VMEM((FIELDS, 16, LANES), f32),
        ],
        in_specs=[hbm] * 5,
        out_specs=[vmem] * 5,
        scratch_shapes=[
            pltpu.VMEM((3, 2) + outer, f32),
            pltpu.VMEM((3, 2) + outer, f32),
            pltpu.SMEM((2, 2, 5), jnp.int32),
            pltpu.VMEM((2, FIELDS, 16, LANES), f32),
            pltpu.VMEM((FIELDS, 16, LANES), f32),
            pltpu.VMEM((FIELDS, 16, LANES), f32),
            pltpu.VMEM((FIELDS, 16, LANES), f32),
            pltpu.VMEM(outer, f32),
            pltpu.VMEM(outer, f32),
            pltpu.VMEM((2, 2, 5), jnp.int32),
            pltpu.VMEM((2, 2, 5), jnp.int32),
            pltpu.SemaphoreType.DMA((5,)),
            pltpu.SemaphoreType.DMA((15,)),
            pltpu.SemaphoreType.DMA((15,)),
            pltpu.SemaphoreType.REGULAR((2,)),
            pltpu.SemaphoreType.REGULAR,
            pltpu.SemaphoreType.REGULAR,
        ],
        compiler_params=pltpu.CompilerParams(collective_id=0, has_side_effects=True),
    )(fine_links, fine, planes, coarse, register)
    updated, faces = pl.pallas_call(
        finish,
        out_shape=[
            jax.ShapeDtypeStruct((2, FIELDS, 256, LANES), f32),
            jax.ShapeDtypeStruct((FIELDS, 16, LANES), f32),
        ],
        in_specs=[vmem] * 5,
        out_specs=[hbm, hbm],
        scratch_shapes=[
            pltpu.VMEM((FIELDS, 64, LANES), f32),
            pltpu.SemaphoreType.DMA((4,)),
        ],
        compiler_params=pltpu.CompilerParams(vmem_limit_bytes=8 * 2**20),
    )(*held)
    updated = updated.reshape(2, FIELDS, 4, 8, 8, LANES).transpose(0, 1, 2, 4, 3, 5)
    faces = faces.reshape(1, FIELDS, 8, 2, LANES).transpose(0, 3, 1, 2, 4)
    return (updated.reshape(2, FIELDS, 32, 1024), faces.reshape(1, 2, FIELDS, 1024))


def solution(mesh):
    in_specs = (
        P(("gx", "gy"), None, None, None),
        P(("gx", "gy"), None, None),
        P(("gx", "gy"), None, None, None, None),
        P(("gx", "gy"), None, None, None),
    )
    out_specs = (P(("gx", "gy"), None, None, None), P(("gx", "gy"), None, None, None))
    return jax.shard_map(shards, mesh=mesh, in_specs=in_specs, out_specs=out_specs, check_vma=False)
```

```python
import jax
import jax.numpy as jnp
from jax import lax
from jax.experimental import pallas as pl
from jax.experimental.pallas import tpu as pltpu
from jax.sharding import PartitionSpec as P

MESH = pl.DeviceIdType.MESH
FIELDS = 5
ROWS, LANES = 8, 128


def plane_rows(x):
    return pl.ds((x // 8) * 64 + x % 8, ROWS, stride=8)


def load_plane(ref, block, x):
    return [ref[block, f, plane_rows(x), :] for f in range(FIELDS)]


def planes_of(ref, x):
    return [ref[f, :, x, 0, :] for f in range(FIELDS)]


def primitive(cell):
    rho, mx, my, mz, energy = cell
    inverse = 1.0 / rho
    u, v, w = mx * inverse, my * inverse, mz * inverse
    p = 0.4 * (energy - 0.5 * (mx * u + my * v + mz * w))
    return [rho, u, v, w, p, inverse]


def edge(w0, w1, w2, w3):
    return [
        (7.0 / 12.0) * (w1[f] + w2[f]) - (1.0 / 12.0) * (w0[f] + w3[f]) for f in range(FIELDS)
    ]


def square_root(x):
    return jnp.sqrt(x)


def states(w, low, high):
    u = w[1]
    c = square_root(1.4 * w[4] * w[5])
    up = 0.1 * jnp.maximum(u + c, 0.0)
    down = 0.1 * jnp.maximum(c - u, 0.0)
    half_up, keep_up = 0.5 * up, 1.0 - (2.0 / 3.0) * up
    half_down, keep_down = 0.5 * down, 1.0 - (2.0 / 3.0) * down
    upper, lower = [], []
    for f in range(FIELDS):
        diff = high[f] - low[f]
        curve = 6.0 * w[f] - 3.0 * (low[f] + high[f])
        upper.append(high[f] - half_up * (diff - keep_up * curve))
        lower.append(low[f] + half_down * (diff + keep_down * curve))
    return upper, lower


def hllc(left, right):
    rho_l, u_l, v_l, w_l, p_l = left
    rho_r, u_r, v_r, w_r, p_r = right
    t_l, t_r = p_l / rho_l, p_r / rho_r
    c_l, c_r = square_root(1.4 * t_l), square_root(1.4 * t_r)
    s_l = jnp.minimum(u_l - c_l, u_r - c_r)
    s_r = jnp.maximum(u_l + c_l, u_r + c_r)
    m_l, m_r = rho_l * (s_l - u_l), rho_r * (s_r - u_r)
    contact = (p_r - p_l + m_l * u_l - m_r * u_r) / (m_l - m_r)
    is_left = jnp.maximum(s_l, contact) >= 0.0

    def pick(a, b):
        return jnp.where(is_left, a, b)

    u, v, w, p, t = (pick(a, b) for a, b in zip((u_l, v_l, w_l, p_l, t_l), (u_r, v_r, w_r, p_r, t_r)))
    m, s = pick(m_l, m_r), pick(s_l, s_r)
    star = pick(-s_l, s_r) > 0.0
    speed = jnp.where(star, contact, u)
    inverse = 1.0 / (s - speed)
    mass = m * inverse * speed
    gap = speed - u
    pressure = p + m * gap
    kinetic = 0.5 * (u * u + v * v + w * w)
    return [
        mass,
        mass * speed + pressure,
        mass * v,
        mass * w,
        mass * (2.5 * t + kinetic + gap * speed) + speed * (gap * p * inverse + pressure),
    ]


def three_fluxes(w):
    a = [edge(w[i], w[i + 1], w[i + 2], w[i + 3]) for i in range(5)]
    sides = [states(w[i + 2], a[i], a[i + 1]) for i in range(4)]
    return [hllc(sides[i][0], sides[i + 1][1]) for i in range(3)]


def iotas():
    return (
        lax.broadcasted_iota(jnp.int32, (ROWS, LANES), 0),
        lax.broadcasted_iota(jnp.int32, (ROWS, LANES), 1),
    )


def prolong(value, q):
    row, lane = iotas()
    rows = (q // 2) * 4 + row // 2
    lanes = ((row % 2) * 2 + lane // 64) * 32 + (q % 2) * 16 + (lane % 32) // 2
    return jnp.take_along_axis(jnp.take_along_axis(value, rows, axis=0), lanes, axis=1)


def patch(flux, q):
    row, lane = iotas()
    total = flux + pltpu.roll(flux, LANES - 1, 1)
    total = total + pltpu.roll(total, LANES - 32, 1)
    lanes = ((lane // 32) % 2) * 64 + 2 * (lane % 16)
    rows = 2 * (row % 4) + lane // 64
    placed = jnp.take_along_axis(jnp.take_along_axis(total, lanes, axis=1), rows, axis=0)
    inside = (row // 4 == q // 2) & ((lane % 32) // 16 == q % 2)
    return jnp.where(inside, 0.125 * placed, 0.0)


def single_flux(w):
    a = [edge(w[i], w[i + 1], w[i + 2], w[i + 3]) for i in range(3)]
    upper, _ = states(w[2], a[0], a[1])
    _, lower = states(w[3], a[1], a[2])
    return hllc(upper, lower)


def coarse_ghosts(ref, side, q):
    near, far = (
        primitive([prolong(ref[f, pl.ds(layer, ROWS, stride=2), :], q) for f in range(FIELDS)])
        for layer in range(2)
    )
    return [far, near, near] if side == 0 else [near, near, far]


def edge_planes(cells, block, side, ghosts, store):
    planes = range(5) if side == 0 else range(27, 32)
    inner = [load_plane(cells, block, x) for x in planes]
    w = [primitive(c) for c in inner]
    fluxes = three_fluxes(ghosts + w if side == 0 else w + ghosts)
    for k, i in enumerate((0, 1) if side == 0 else (3, 4)):
        for f in range(FIELDS):
            store(f, planes[i], inner[i][f] - 0.1 * (fluxes[k + 1][f] - fluxes[k][f]))
    return (fluxes[0], fluxes[2]) if side == 0 else (fluxes[2], fluxes[0])


def bulk(cells, out, kept, block):
    first = [load_plane(cells, block, x) for x in range(6)]
    w = [primitive(c) for c in first]
    a = [edge(w[i], w[i + 1], w[i + 2], w[i + 3]) for i in range(3)]
    upper2, _ = states(w[2], a[0], a[1])
    upper3, lower3 = states(w[3], a[1], a[2])
    flux3 = hllc(upper2, lower3)
    for f in range(FIELDS):
        kept[block, 0, f] = flux3[f]

    def step(i, carry):
        w0, w1, w2, low, upper, flux = carry
        w3 = primitive(load_plane(cells, block, i + 2))
        high = edge(w0, w1, w2, w3)
        next_upper, lower = states(w1, low, high)
        next_flux = hllc(upper, lower)
        here = plane_rows(i - 1)
        for f in range(FIELDS):
            out[block, f, here, :] = cells[block, f, here, :] - 0.1 * (next_flux[f] - flux[f])
        return w1, w2, w3, high, next_upper, next_flux

    carry = (w[3], w[4], w[5], a[2], upper3, flux3)
    carry = lax.fori_loop(0, 13, lambda k, c: step(5 + 2 * k, step(4 + 2 * k, c)), carry)
    for f in range(FIELDS):
        kept[block, 1, f] = carry[5][f]


def block_one_edge(side, ghost_planes, cells, kept, store):
    ghosts = [primitive(plane) for plane in ghost_planes]
    _, third = edge_planes(cells, 1, side, ghosts, store)
    x = 2 if side == 0 else 29
    for f in range(FIELDS):
        change = kept[1, 0, f] - third[f] if side == 0 else third[f] - kept[1, 1, f]
        store(f, x, cells[1, f, plane_rows(x), :] - 0.1 * change)


def exchange(
    n_gx, n_gy, links_in, fine, planes, coarse, register,
    out, cells, low_ghosts, kept, faces_out,
    from_below, from_above, links, own_coarse, own_register,
    coarse_below, coarse_above, low_below, high_above, links_below, links_above,
    local_sem, send_sem, recv_sem, relay_sem, beside_sem, below_sem,
):
    gx, gy = lax.axis_index("gx"), lax.axis_index("gy")
    above = (lax.rem(gx + 1, n_gx), gy)
    below = (lax.rem(gx + n_gx - 1, n_gx), gy)
    right = (gx, lax.rem(gy + 1, n_gy))
    left = (gx, lax.rem(gy + n_gy - 1, n_gy))
    odd = lax.rem(gy, 2) == 1
    is_first = gx == 0
    is_last = gx == n_gx - 1

    def fetch(src, dst, k):
        copy = pltpu.make_async_copy(src, dst, local_sem.at[k])
        copy.start()
        return copy

    def signal(semaphore, device):
        pl.semaphore_signal(semaphore, inc=1, device_id=device, device_id_type=MESH)

    barrier = pltpu.get_barrier_semaphore()
    signal(barrier, below)

    @pl.when(odd)
    def _():
        signal(barrier, (below[0], right[1]))

    @pl.when(jnp.logical_not(is_last))
    def _():
        signal(barrier, right)
        signal(barrier, left)

    pl.semaphore_wait(barrier, jnp.where(is_last, 1, 3) + jnp.where(odd, 0, 1))

    def remote(src, dst, device, k):
        return pltpu.make_async_remote_copy(
            src_ref=src, dst_ref=dst, send_sem=send_sem.at[k], recv_sem=recv_sem.at[k],
            device_id=device, device_id_type=MESH,
        )

    def high(b):
        return planes.at[b, :, 3, :, pl.ds(5, 3)]

    def low(b):
        return planes.at[b, :, 0, :, pl.ds(0, 3)]

    parts = [(0, pl.ds(0, 3)), (0, pl.ds(3, 2)), (1, pl.ds(0, 5))]

    def part(index, column):
        b, fields = parts[index]
        return from_below.at[column, b, fields]

    fine_up = [
        remote(planes.at[b, fields, 3, :, pl.ds(5, 3)], part(k, 1), above, (0, 1, 15)[k])
        for k, (b, fields) in enumerate(parts)
    ]
    coarse_up = remote(coarse.at[0], coarse_below, above, 2)
    low_up = remote(low(0), low_below, above, 3)
    links_up = remote(links_in, links_below, above, 4)
    coarse_down = remote(coarse.at[1], coarse_above, below, 5)
    fine_down = remote(planes.at[:, :, 0, :, pl.ds(0, 3)], from_above.at[1], below, 6)
    high_down = remote(high(0), high_above, below, 7)
    links_down = remote(links_in, links_above, below, 8)
    across_up = remote(high(1), from_below.at[2, 1], (above[0], left[1]), 12)
    on_up = [
        [remote(part(k, 1), part(k, 0), right, r), remote(part(k, 1), part(k, 2), left, l)]
        for k, (r, l) in enumerate(((9, 10), (16, 17), (11, 12)))
    ]
    on_down = [
        remote(from_above.at[1], from_above.at[0], right, 13),
        remote(from_above.at[1], from_above.at[2], left, 14),
    ]

    for copy in fine_up:
        copy.start()

    @pl.when(jnp.logical_not(odd))
    def _():
        across_up.start()

    signal(below_sem, above)
    cells_in = [fetch(fine.at[b], cells.at[b], b) for b in range(2)]
    links_copy = fetch(links_in, links, 2)
    coarse_in = fetch(coarse, own_coarse, 3)
    register_in = fetch(register, own_register, 4)
    cells_in[0].wait()
    bulk(cells, out, kept, 0)
    for copy in fine_up:
        copy.wait_send()
    coarse_up.start()
    low_up.start()
    links_up.start()
    cells_in[1].wait()
    bulk(cells, out, kept, 1)

    def forward_down():
        fine_down.wait_recv()
        for copy in on_down:
            copy.start()

    def send_down():
        for copy in (coarse_down, fine_down, high_down, links_down):
            copy.start()

    @pl.when(is_first)
    def _():
        forward_down()

    pl.semaphore_wait(below_sem, 1)
    send_down()

    @pl.when(is_first)
    def _():
        signal(relay_sem.at[0], right)
        signal(relay_sem.at[1], left)

    @pl.when(is_last)
    def _():
        pl.semaphore_wait(beside_sem, 1)

    for k in range(2):
        fine_up[k].wait_recv()
        for copy in on_up[k]:
            copy.start()
    fine_up[2].wait_recv()
    on_up[2][0].start()

    @pl.when(odd)
    def _():
        on_up[2][1].start()


    @pl.when(is_first)
    def _():
        pl.semaphore_wait(relay_sem.at[0], 1)
        pl.semaphore_wait(relay_sem.at[1], 1)
        signal(beside_sem, below)

    @pl.when(jnp.logical_not(is_first))
    def _():
        forward_down()

    def store(f, x, value):
        out[0, f, plane_rows(x), :] = value

    def block_zero_edge(side):
        ghosts = coarse_ghosts(coarse_above if side == 0 else coarse_below, side, links[0, side, 4])
        _, third = edge_planes(cells, 0, side, ghosts, store)
        x = 2 if side == 0 else 29
        for f in range(FIELDS):
            change = kept[0, 0, f] - third[f] if side == 0 else third[f] - kept[0, 1, f]
            store(f, x, cells[0, f, plane_rows(x), :] - 0.1 * change)

    def coarse_face(t):
        side = 1 - t
        their_links = links_below if side == 0 else links_above
        q = jnp.broadcast_to(their_links[0][side : side + 1, 4:5], (ROWS, LANES))
        outer = low_below if side == 0 else high_above
        ghosts = coarse_ghosts(own_coarse.at[t], side, q)
        w = [primitive(planes_of(outer, x)) for x in range(3)]
        flux = single_flux(ghosts + w if side == 0 else w + ghosts)
        factor = 0.05 if t == 0 else -0.05
        here = pl.ds(t, ROWS, stride=2)
        for f in range(FIELDS):
            faces_out[f, here, :] = own_coarse[t, f, pl.ds(0, ROWS, stride=2), :] + factor * (
                own_register[f, here, :] + patch(flux[f], q)
            )

    def store_one(f, x, value):
        out[1, f, plane_rows(x), :] = value

    links_copy.wait()
    coarse_in.wait()
    register_in.wait()
    coarse_down.wait_recv()
    block_zero_edge(0)
    for copy in (high_down, links_down):
        copy.wait_recv()
    coarse_face(0)
    for copy in on_down:
        copy.wait_recv()
    column, slot = links[1, 1, 2], links[1, 1, 3]
    ghost_planes = [planes_of(from_above.at[column, slot], x) for x in range(3)]
    block_one_edge(1, ghost_planes, cells, kept, store_one)
    coarse_up.wait_recv()
    block_zero_edge(1)
    for copy in (low_up, links_up):
        copy.wait_recv()
    coarse_face(1)

    for copy in (coarse_up, low_up, links_up, coarse_down, fine_down, high_down, links_down):
        copy.wait_send()
    for copy in on_down + on_up[0] + on_up[1] + on_up[2]:
        copy.wait_send()

    for copy in on_up[0] + on_up[1] + on_up[2]:
        copy.wait_recv()
    column, slot = links[1, 0, 2], links[1, 0, 3]
    for x in range(3):
        for f, value in enumerate(planes_of(from_below.at[column, slot], x)):
            low_ghosts[f, x] = value


def finish(done, cells, low_ghosts, kept, faces, out, faces_out, tile, sem):
    def put(src, dst, k):
        copy = pltpu.make_async_copy(src, dst, sem.at[k])
        copy.start()
        return copy

    copies = [
        put(done.at[0], out.at[0], 0),
        put(done.at[1, :, pl.ds(64, 192), :], out.at[1, :, pl.ds(64, 192), :], 1),
        put(faces, faces_out, 2),
    ]

    def store(f, x, value):
        tile[f, pl.ds(x, ROWS, stride=8), :] = value

    ghost_planes = [[low_ghosts[f, x] for f in range(FIELDS)] for x in range(3)]
    block_one_edge(0, ghost_planes, cells, kept, store)
    for f in range(FIELDS):
        for x in range(3, 8):
            store(f, x, done[1, f, plane_rows(x), :])
    copies.append(put(tile, out.at[1, :, pl.ds(0, 64), :], 3))
    for copy in copies:
        copy.wait()


def shards(fine_state, fine_links, coarse_edges, flux_register):
    n_gx, n_gy = lax.axis_size("gx"), lax.axis_size("gy")
    f32 = jnp.float32
    fine = fine_state.reshape(2, FIELDS, 4, 8, 8, LANES).transpose(0, 1, 2, 4, 3, 5)
    planes = fine.reshape(2, FIELDS, 4, 8, 8, 1, LANES)
    fine = fine.reshape(2, FIELDS, 256, LANES)
    coarse = coarse_edges.reshape(2, FIELDS, 2, 8, LANES).transpose(0, 1, 3, 2, 4)
    coarse = coarse.reshape(2, FIELDS, 16, LANES)
    register = flux_register.reshape(2, FIELDS, 8, LANES).transpose(1, 2, 0, 3)
    register = register.reshape(FIELDS, 16, LANES)
    plane = (ROWS, LANES)
    outer = (FIELDS, ROWS, 3, 1, LANES)
    hbm = pl.BlockSpec(memory_space=pltpu.HBM)
    vmem = pl.BlockSpec(memory_space=pltpu.VMEM)
    held = pl.pallas_call(
        lambda *refs: exchange(n_gx, n_gy, *refs),
        out_shape=[
            pltpu.VMEM((2, FIELDS, 256, LANES), f32),
            pltpu.VMEM((2, FIELDS, 256, LANES), f32),
            pltpu.VMEM((FIELDS, 3) + plane, f32),
            pltpu.VMEM((2, 2, FIELDS) + plane, f32),
            pltpu.VMEM((FIELDS, 16, LANES), f32),
        ],
        in_specs=[hbm] * 5,
        out_specs=[vmem] * 5,
        scratch_shapes=[
            pltpu.VMEM((3, 2) + outer, f32),
            pltpu.VMEM((3, 2) + outer, f32),
            pltpu.SMEM((2, 2, 5), jnp.int32),
            pltpu.VMEM((2, FIELDS, 16, LANES), f32),
            pltpu.VMEM((FIELDS, 16, LANES), f32),
            pltpu.VMEM((FIELDS, 16, LANES), f32),
            pltpu.VMEM((FIELDS, 16, LANES), f32),
            pltpu.VMEM(outer, f32),
            pltpu.VMEM(outer, f32),
            pltpu.VMEM((2, 2, 5), jnp.int32),
            pltpu.VMEM((2, 2, 5), jnp.int32),
            pltpu.SemaphoreType.DMA((5,)),
            pltpu.SemaphoreType.DMA((18,)),
            pltpu.SemaphoreType.DMA((18,)),
            pltpu.SemaphoreType.REGULAR((2,)),
            pltpu.SemaphoreType.REGULAR,
            pltpu.SemaphoreType.REGULAR,
        ],
        compiler_params=pltpu.CompilerParams(collective_id=0, has_side_effects=True),
    )(fine_links, fine, planes, coarse, register)
    updated, faces = pl.pallas_call(
        finish,
        out_shape=[
            jax.ShapeDtypeStruct((2, FIELDS, 256, LANES), f32),
            jax.ShapeDtypeStruct((FIELDS, 16, LANES), f32),
        ],
        in_specs=[vmem] * 5,
        out_specs=[hbm, hbm],
        scratch_shapes=[
            pltpu.VMEM((FIELDS, 64, LANES), f32),
            pltpu.SemaphoreType.DMA((4,)),
        ],
        compiler_params=pltpu.CompilerParams(vmem_limit_bytes=8 * 2**20),
    )(*held)
    updated = updated.reshape(2, FIELDS, 4, 8, 8, LANES).transpose(0, 1, 2, 4, 3, 5)
    faces = faces.reshape(1, FIELDS, 8, 2, LANES).transpose(0, 3, 1, 2, 4)
    return (updated.reshape(2, FIELDS, 32, 1024), faces.reshape(1, 2, FIELDS, 1024))


def solution(mesh):
    in_specs = (
        P(("gx", "gy"), None, None, None),
        P(("gx", "gy"), None, None),
        P(("gx", "gy"), None, None, None, None),
        P(("gx", "gy"), None, None, None),
    )
    out_specs = (P(("gx", "gy"), None, None, None), P(("gx", "gy"), None, None, None))
    return jax.shard_map(shards, mesh=mesh, in_specs=in_specs, out_specs=out_specs, check_vma=False)
```

```python
import jax
import jax.numpy as jnp
from jax import lax
from jax.experimental import pallas as pl
from jax.experimental.pallas import tpu as pltpu
from jax.sharding import PartitionSpec as P

MESH = pl.DeviceIdType.MESH
FIELDS = 5
ROWS, LANES = 8, 128


def plane_rows(x):
    return pl.ds((x // 8) * 64 + x % 8, ROWS, stride=8)


def load_plane(ref, block, x):
    return [ref[block, f, plane_rows(x), :] for f in range(FIELDS)]


def planes_of(ref, x):
    return [ref[f, :, x, 0, :] for f in range(FIELDS)]


def primitive(cell):
    rho, mx, my, mz, energy = cell
    inverse = 1.0 / rho
    u, v, w = mx * inverse, my * inverse, mz * inverse
    p = 0.4 * (energy - 0.5 * (mx * u + my * v + mz * w))
    return [rho, u, v, w, p, inverse]


def edge(w0, w1, w2, w3):
    return [
        (7.0 / 12.0) * (w1[f] + w2[f]) - (1.0 / 12.0) * (w0[f] + w3[f]) for f in range(FIELDS)
    ]


def square_root(x):
    return jnp.sqrt(x)


def states(w, low, high):
    u = w[1]
    c = square_root(1.4 * w[4] * w[5])
    up = 0.1 * jnp.maximum(u + c, 0.0)
    down = 0.1 * jnp.maximum(c - u, 0.0)
    half_up, keep_up = 0.5 * up, 1.0 - (2.0 / 3.0) * up
    half_down, keep_down = 0.5 * down, 1.0 - (2.0 / 3.0) * down
    upper, lower = [], []
    for f in range(FIELDS):
        diff = high[f] - low[f]
        curve = 6.0 * w[f] - 3.0 * (low[f] + high[f])
        upper.append(high[f] - half_up * (diff - keep_up * curve))
        lower.append(low[f] + half_down * (diff + keep_down * curve))
    return upper, lower


def hllc(left, right):
    rho_l, u_l, v_l, w_l, p_l = left
    rho_r, u_r, v_r, w_r, p_r = right
    t_l, t_r = p_l / rho_l, p_r / rho_r
    c_l, c_r = square_root(1.4 * t_l), square_root(1.4 * t_r)
    s_l = jnp.minimum(u_l - c_l, u_r - c_r)
    s_r = jnp.maximum(u_l + c_l, u_r + c_r)
    m_l, m_r = rho_l * (s_l - u_l), rho_r * (s_r - u_r)
    contact = (p_r - p_l + m_l * u_l - m_r * u_r) / (m_l - m_r)
    is_left = jnp.maximum(s_l, contact) >= 0.0

    def pick(a, b):
        return jnp.where(is_left, a, b)

    u, v, w, p, t = (pick(a, b) for a, b in zip((u_l, v_l, w_l, p_l, t_l), (u_r, v_r, w_r, p_r, t_r)))
    m, s = pick(m_l, m_r), pick(s_l, s_r)
    star = pick(-s_l, s_r) > 0.0
    speed = jnp.where(star, contact, u)
    inverse = 1.0 / (s - speed)
    mass = m * inverse * speed
    gap = speed - u
    pressure = p + m * gap
    kinetic = 0.5 * (u * u + v * v + w * w)
    return [
        mass,
        mass * speed + pressure,
        mass * v,
        mass * w,
        mass * (2.5 * t + kinetic + gap * speed) + speed * (gap * p * inverse + pressure),
    ]


def three_fluxes(w):
    a = [edge(w[i], w[i + 1], w[i + 2], w[i + 3]) for i in range(5)]
    sides = [states(w[i + 2], a[i], a[i + 1]) for i in range(4)]
    return [hllc(sides[i][0], sides[i + 1][1]) for i in range(3)]


def iotas():
    return (
        lax.broadcasted_iota(jnp.int32, (ROWS, LANES), 0),
        lax.broadcasted_iota(jnp.int32, (ROWS, LANES), 1),
    )


def prolong(value, q):
    row, lane = iotas()
    rows = (q // 2) * 4 + row // 2
    lanes = ((row % 2) * 2 + lane // 64) * 32 + (q % 2) * 16 + (lane % 32) // 2
    return jnp.take_along_axis(jnp.take_along_axis(value, rows, axis=0), lanes, axis=1)


def patch(flux, q):
    row, lane = iotas()
    total = flux + pltpu.roll(flux, LANES - 1, 1)
    total = total + pltpu.roll(total, LANES - 32, 1)
    lanes = ((lane // 32) % 2) * 64 + 2 * (lane % 16)
    rows = 2 * (row % 4) + lane // 64
    placed = jnp.take_along_axis(jnp.take_along_axis(total, lanes, axis=1), rows, axis=0)
    inside = (row // 4 == q // 2) & ((lane % 32) // 16 == q % 2)
    return jnp.where(inside, 0.125 * placed, 0.0)


def single_flux(w):
    a = [edge(w[i], w[i + 1], w[i + 2], w[i + 3]) for i in range(3)]
    upper, _ = states(w[2], a[0], a[1])
    _, lower = states(w[3], a[1], a[2])
    return hllc(upper, lower)


def coarse_ghosts(ref, side, q):
    near, far = (
        primitive([prolong(ref[f, pl.ds(layer, ROWS, stride=2), :], q) for f in range(FIELDS)])
        for layer in range(2)
    )
    return [far, near, near] if side == 0 else [near, near, far]


def edge_planes(cells, block, side, ghosts, store):
    planes = range(5) if side == 0 else range(27, 32)
    inner = [load_plane(cells, block, x) for x in planes]
    w = [primitive(c) for c in inner]
    fluxes = three_fluxes(ghosts + w if side == 0 else w + ghosts)
    for k, i in enumerate((0, 1) if side == 0 else (3, 4)):
        for f in range(FIELDS):
            store(f, planes[i], inner[i][f] - 0.1 * (fluxes[k + 1][f] - fluxes[k][f]))
    return (fluxes[0], fluxes[2]) if side == 0 else (fluxes[2], fluxes[0])


def bulk(cells, out, kept, block):
    first = [load_plane(cells, block, x) for x in range(6)]
    w = [primitive(c) for c in first]
    a = [edge(w[i], w[i + 1], w[i + 2], w[i + 3]) for i in range(3)]
    upper2, _ = states(w[2], a[0], a[1])
    upper3, lower3 = states(w[3], a[1], a[2])
    flux3 = hllc(upper2, lower3)
    for f in range(FIELDS):
        kept[block, 0, f] = flux3[f]

    def step(i, carry):
        w0, w1, w2, low, upper, flux = carry
        w3 = primitive(load_plane(cells, block, i + 2))
        high = edge(w0, w1, w2, w3)
        next_upper, lower = states(w1, low, high)
        next_flux = hllc(upper, lower)
        here = plane_rows(i - 1)
        for f in range(FIELDS):
            out[block, f, here, :] = cells[block, f, here, :] - 0.1 * (next_flux[f] - flux[f])
        return w1, w2, w3, high, next_upper, next_flux

    carry = (w[3], w[4], w[5], a[2], upper3, flux3)
    carry = lax.fori_loop(0, 13, lambda k, c: step(5 + 2 * k, step(4 + 2 * k, c)), carry)
    for f in range(FIELDS):
        kept[block, 1, f] = carry[5][f]


def block_one_edge(side, ghost_planes, cells, kept, store):
    ghosts = [primitive(plane) for plane in ghost_planes]
    _, third = edge_planes(cells, 1, side, ghosts, store)
    x = 2 if side == 0 else 29
    for f in range(FIELDS):
        change = kept[1, 0, f] - third[f] if side == 0 else third[f] - kept[1, 1, f]
        store(f, x, cells[1, f, plane_rows(x), :] - 0.1 * change)


def exchange(
    n_gx, n_gy, links_in, fine, planes, coarse, register,
    out, cells, low_ghosts, kept, faces_out,
    from_below, from_above, links, own_coarse, own_register,
    coarse_below, coarse_above, low_below, high_above, links_below, links_above,
    local_sem, send_sem, recv_sem, relay_sem, beside_sem, below_sem,
):
    gx, gy = lax.axis_index("gx"), lax.axis_index("gy")
    above = (lax.rem(gx + 1, n_gx), gy)
    below = (lax.rem(gx + n_gx - 1, n_gx), gy)
    right = (gx, lax.rem(gy + 1, n_gy))
    left = (gx, lax.rem(gy + n_gy - 1, n_gy))
    odd = lax.rem(gy, 2) == 1
    is_first = gx == 0
    is_last = gx == n_gx - 1

    def fetch(src, dst, k):
        copy = pltpu.make_async_copy(src, dst, local_sem.at[k])
        copy.start()
        return copy

    def signal(semaphore, device):
        pl.semaphore_signal(semaphore, inc=1, device_id=device, device_id_type=MESH)

    barrier = pltpu.get_barrier_semaphore()
    signal(barrier, below)

    @pl.when(odd)
    def _():
        signal(barrier, (below[0], right[1]))

    @pl.when(jnp.logical_not(is_last))
    def _():
        signal(barrier, right)
        signal(barrier, left)

    pl.semaphore_wait(barrier, jnp.where(is_last, 1, 3) + jnp.where(odd, 0, 1))

    def remote(src, dst, device, k):
        return pltpu.make_async_remote_copy(
            src_ref=src, dst_ref=dst, send_sem=send_sem.at[k], recv_sem=recv_sem.at[k],
            device_id=device, device_id_type=MESH,
        )

    def high(b):
        return planes.at[b, :, 3, :, pl.ds(5, 3)]

    def low(b):
        return planes.at[b, :, 0, :, pl.ds(0, 3)]

    parts = [(0, pl.ds(0, 3)), (0, pl.ds(3, 2)), (1, pl.ds(0, 5))]

    def part(index, column):
        b, fields = parts[index]
        return from_below.at[column, b, fields]

    fine_up = [
        remote(planes.at[b, fields, 3, :, pl.ds(5, 3)], part(k, 1), above, (0, 1, 15)[k])
        for k, (b, fields) in enumerate(parts)
    ]
    coarse_up = remote(coarse.at[0], coarse_below, above, 2)
    low_up = remote(low(0), low_below, above, 3)
    links_up = remote(links_in, links_below, above, 4)
    coarse_down = remote(coarse.at[1], coarse_above, below, 5)
    fine_down = remote(planes.at[:, :, 0, :, pl.ds(0, 3)], from_above.at[1], below, 6)
    high_down = remote(high(0), high_above, below, 7)
    links_down = remote(links_in, links_above, below, 8)
    across_up = remote(high(1), from_below.at[2, 1], (above[0], left[1]), 12)
    on_up = [
        [remote(part(k, 1), part(k, 0), right, r), remote(part(k, 1), part(k, 2), left, l)]
        for k, (r, l) in enumerate(((9, 10), (16, 17), (11, 12)))
    ]
    on_down = [
        remote(from_above.at[1], from_above.at[0], right, 13),
        remote(from_above.at[1], from_above.at[2], left, 14),
    ]

    for copy in fine_up:
        copy.start()

    @pl.when(jnp.logical_not(odd))
    def _():
        across_up.start()

    signal(below_sem, above)
    cells_in = [fetch(fine.at[b], cells.at[b], b) for b in range(2)]
    links_copy = fetch(links_in, links, 2)
    coarse_in = fetch(coarse, own_coarse, 3)
    register_in = fetch(register, own_register, 4)
    cells_in[0].wait()
    bulk(cells, out, kept, 0)
    for copy in fine_up:
        copy.wait_send()
    coarse_up.start()
    low_up.start()
    links_up.start()
    cells_in[1].wait()
    bulk(cells, out, kept, 1)

    def forward_down():
        fine_down.wait_recv()
        for copy in on_down:
            copy.start()

    def send_down():
        for copy in (coarse_down, fine_down, high_down, links_down):
            copy.start()

    @pl.when(is_first)
    def _():
        forward_down()

    pl.semaphore_wait(below_sem, 1)
    send_down()

    @pl.when(is_first)
    def _():
        signal(relay_sem.at[0], right)
        signal(relay_sem.at[1], left)

    @pl.when(is_last)
    def _():
        pl.semaphore_wait(beside_sem, 1)

    for k in range(2):
        fine_up[k].wait_recv()
        on_up[k][1].start()
        on_up[k][0].start()
    fine_up[2].wait_recv()
    on_up[2][0].start()

    @pl.when(odd)
    def _():
        on_up[2][1].start()


    @pl.when(is_first)
    def _():
        pl.semaphore_wait(relay_sem.at[0], 1)
        pl.semaphore_wait(relay_sem.at[1], 1)
        signal(beside_sem, below)

    @pl.when(jnp.logical_not(is_first))
    def _():
        forward_down()

    def store(f, x, value):
        out[0, f, plane_rows(x), :] = value

    def block_zero_edge(side):
        ghosts = coarse_ghosts(coarse_above if side == 0 else coarse_below, side, links[0, side, 4])
        _, third = edge_planes(cells, 0, side, ghosts, store)
        x = 2 if side == 0 else 29
        for f in range(FIELDS):
            change = kept[0, 0, f] - third[f] if side == 0 else third[f] - kept[0, 1, f]
            store(f, x, cells[0, f, plane_rows(x), :] - 0.1 * change)

    def coarse_face(t):
        side = 1 - t
        their_links = links_below if side == 0 else links_above
        q = jnp.broadcast_to(their_links[0][side : side + 1, 4:5], (ROWS, LANES))
        outer = low_below if side == 0 else high_above
        ghosts = coarse_ghosts(own_coarse.at[t], side, q)
        w = [primitive(planes_of(outer, x)) for x in range(3)]
        flux = single_flux(ghosts + w if side == 0 else w + ghosts)
        factor = 0.05 if t == 0 else -0.05
        here = pl.ds(t, ROWS, stride=2)
        for f in range(FIELDS):
            faces_out[f, here, :] = own_coarse[t, f, pl.ds(0, ROWS, stride=2), :] + factor * (
                own_register[f, here, :] + patch(flux[f], q)
            )

    def store_one(f, x, value):
        out[1, f, plane_rows(x), :] = value

    links_copy.wait()
    coarse_in.wait()
    register_in.wait()
    coarse_down.wait_recv()
    block_zero_edge(0)
    for copy in (high_down, links_down):
        copy.wait_recv()
    coarse_face(0)
    for copy in on_down:
        copy.wait_recv()
    column, slot = links[1, 1, 2], links[1, 1, 3]
    ghost_planes = [planes_of(from_above.at[column, slot], x) for x in range(3)]
    block_one_edge(1, ghost_planes, cells, kept, store_one)
    coarse_up.wait_recv()
    block_zero_edge(1)
    for copy in (low_up, links_up):
        copy.wait_recv()
    coarse_face(1)

    for copy in (coarse_up, low_up, links_up, coarse_down, fine_down, high_down, links_down):
        copy.wait_send()
    for copy in on_down + on_up[0] + on_up[1] + on_up[2]:
        copy.wait_send()

    for copy in on_up[0] + on_up[1] + on_up[2]:
        copy.wait_recv()
    column, slot = links[1, 0, 2], links[1, 0, 3]
    for x in range(3):
        for f, value in enumerate(planes_of(from_below.at[column, slot], x)):
            low_ghosts[f, x] = value


def finish(done, cells, low_ghosts, kept, faces, out, faces_out, tile, sem):
    def put(src, dst, k):
        copy = pltpu.make_async_copy(src, dst, sem.at[k])
        copy.start()
        return copy

    copies = [
        put(done.at[0], out.at[0], 0),
        put(done.at[1, :, pl.ds(64, 192), :], out.at[1, :, pl.ds(64, 192), :], 1),
        put(faces, faces_out, 2),
    ]

    def store(f, x, value):
        tile[f, pl.ds(x, ROWS, stride=8), :] = value

    ghost_planes = [[low_ghosts[f, x] for f in range(FIELDS)] for x in range(3)]
    block_one_edge(0, ghost_planes, cells, kept, store)
    for f in range(FIELDS):
        for x in range(3, 8):
            store(f, x, done[1, f, plane_rows(x), :])
    copies.append(put(tile, out.at[1, :, pl.ds(0, 64), :], 3))
    for copy in copies:
        copy.wait()


def shards(fine_state, fine_links, coarse_edges, flux_register):
    n_gx, n_gy = lax.axis_size("gx"), lax.axis_size("gy")
    f32 = jnp.float32
    fine = fine_state.reshape(2, FIELDS, 4, 8, 8, LANES).transpose(0, 1, 2, 4, 3, 5)
    planes = fine.reshape(2, FIELDS, 4, 8, 8, 1, LANES)
    fine = fine.reshape(2, FIELDS, 256, LANES)
    coarse = coarse_edges.reshape(2, FIELDS, 2, 8, LANES).transpose(0, 1, 3, 2, 4)
    coarse = coarse.reshape(2, FIELDS, 16, LANES)
    register = flux_register.reshape(2, FIELDS, 8, LANES).transpose(1, 2, 0, 3)
    register = register.reshape(FIELDS, 16, LANES)
    plane = (ROWS, LANES)
    outer = (FIELDS, ROWS, 3, 1, LANES)
    hbm = pl.BlockSpec(memory_space=pltpu.HBM)
    vmem = pl.BlockSpec(memory_space=pltpu.VMEM)
    held = pl.pallas_call(
        lambda *refs: exchange(n_gx, n_gy, *refs),
        out_shape=[
            pltpu.VMEM((2, FIELDS, 256, LANES), f32),
            pltpu.VMEM((2, FIELDS, 256, LANES), f32),
            pltpu.VMEM((FIELDS, 3) + plane, f32),
            pltpu.VMEM((2, 2, FIELDS) + plane, f32),
            pltpu.VMEM((FIELDS, 16, LANES), f32),
        ],
        in_specs=[hbm] * 5,
        out_specs=[vmem] * 5,
        scratch_shapes=[
            pltpu.VMEM((3, 2) + outer, f32),
            pltpu.VMEM((3, 2) + outer, f32),
            pltpu.SMEM((2, 2, 5), jnp.int32),
            pltpu.VMEM((2, FIELDS, 16, LANES), f32),
            pltpu.VMEM((FIELDS, 16, LANES), f32),
            pltpu.VMEM((FIELDS, 16, LANES), f32),
            pltpu.VMEM((FIELDS, 16, LANES), f32),
            pltpu.VMEM(outer, f32),
            pltpu.VMEM(outer, f32),
            pltpu.VMEM((2, 2, 5), jnp.int32),
            pltpu.VMEM((2, 2, 5), jnp.int32),
            pltpu.SemaphoreType.DMA((5,)),
            pltpu.SemaphoreType.DMA((18,)),
            pltpu.SemaphoreType.DMA((18,)),
            pltpu.SemaphoreType.REGULAR((2,)),
            pltpu.SemaphoreType.REGULAR,
            pltpu.SemaphoreType.REGULAR,
        ],
        compiler_params=pltpu.CompilerParams(collective_id=0, has_side_effects=True),
    )(fine_links, fine, planes, coarse, register)
    updated, faces = pl.pallas_call(
        finish,
        out_shape=[
            jax.ShapeDtypeStruct((2, FIELDS, 256, LANES), f32),
            jax.ShapeDtypeStruct((FIELDS, 16, LANES), f32),
        ],
        in_specs=[vmem] * 5,
        out_specs=[hbm, hbm],
        scratch_shapes=[
            pltpu.VMEM((FIELDS, 64, LANES), f32),
            pltpu.SemaphoreType.DMA((4,)),
        ],
        compiler_params=pltpu.CompilerParams(vmem_limit_bytes=8 * 2**20),
    )(*held)
    updated = updated.reshape(2, FIELDS, 4, 8, 8, LANES).transpose(0, 1, 2, 4, 3, 5)
    faces = faces.reshape(1, FIELDS, 8, 2, LANES).transpose(0, 3, 1, 2, 4)
    return (updated.reshape(2, FIELDS, 32, 1024), faces.reshape(1, 2, FIELDS, 1024))


def solution(mesh):
    in_specs = (
        P(("gx", "gy"), None, None, None),
        P(("gx", "gy"), None, None),
        P(("gx", "gy"), None, None, None, None),
        P(("gx", "gy"), None, None, None),
    )
    out_specs = (P(("gx", "gy"), None, None, None), P(("gx", "gy"), None, None, None))
    return jax.shard_map(shards, mesh=mesh, in_specs=in_specs, out_specs=out_specs, check_vma=False)
```

```python
import jax
import jax.numpy as jnp
from jax import lax
from jax.experimental import pallas as pl
from jax.experimental.pallas import tpu as pltpu
from jax.sharding import PartitionSpec as P

MESH = pl.DeviceIdType.MESH
FIELDS = 5
ROWS, LANES = 8, 128


def plane_rows(x):
    return pl.ds((x // 8) * 64 + x % 8, ROWS, stride=8)


def load_plane(ref, block, x):
    return [ref[block, f, plane_rows(x), :] for f in range(FIELDS)]


def planes_of(ref, x):
    return [ref[f, :, x, 0, :] for f in range(FIELDS)]


def primitive(cell):
    rho, mx, my, mz, energy = cell
    inverse = 1.0 / rho
    u, v, w = mx * inverse, my * inverse, mz * inverse
    p = 0.4 * (energy - 0.5 * (mx * u + my * v + mz * w))
    return [rho, u, v, w, p, inverse]


def edge(w0, w1, w2, w3):
    return [
        (7.0 / 12.0) * (w1[f] + w2[f]) - (1.0 / 12.0) * (w0[f] + w3[f]) for f in range(FIELDS)
    ]


def square_root(x):
    return jnp.sqrt(x)


def states(w, low, high):
    u = w[1]
    c = square_root(1.4 * w[4] * w[5])
    up = 0.1 * jnp.maximum(u + c, 0.0)
    down = 0.1 * jnp.maximum(c - u, 0.0)
    half_up, keep_up = 0.5 * up, 1.0 - (2.0 / 3.0) * up
    half_down, keep_down = 0.5 * down, 1.0 - (2.0 / 3.0) * down
    upper, lower = [], []
    for f in range(FIELDS):
        diff = high[f] - low[f]
        curve = 6.0 * w[f] - 3.0 * (low[f] + high[f])
        upper.append(high[f] - half_up * (diff - keep_up * curve))
        lower.append(low[f] + half_down * (diff + keep_down * curve))
    return upper, lower


def hllc(left, right):
    rho_l, u_l, v_l, w_l, p_l = left
    rho_r, u_r, v_r, w_r, p_r = right
    t_l, t_r = p_l / rho_l, p_r / rho_r
    c_l, c_r = square_root(1.4 * t_l), square_root(1.4 * t_r)
    s_l = jnp.minimum(u_l - c_l, u_r - c_r)
    s_r = jnp.maximum(u_l + c_l, u_r + c_r)
    m_l, m_r = rho_l * (s_l - u_l), rho_r * (s_r - u_r)
    contact = (p_r - p_l + m_l * u_l - m_r * u_r) / (m_l - m_r)
    is_left = jnp.maximum(s_l, contact) >= 0.0

    def pick(a, b):
        return jnp.where(is_left, a, b)

    u, v, w, p, t = (pick(a, b) for a, b in zip((u_l, v_l, w_l, p_l, t_l), (u_r, v_r, w_r, p_r, t_r)))
    m, s = pick(m_l, m_r), pick(s_l, s_r)
    star = pick(-s_l, s_r) > 0.0
    speed = jnp.where(star, contact, u)
    inverse = 1.0 / (s - speed)
    mass = m * inverse * speed
    gap = speed - u
    pressure = p + m * gap
    kinetic = 0.5 * (u * u + v * v + w * w)
    return [
        mass,
        mass * speed + pressure,
        mass * v,
        mass * w,
        mass * (2.5 * t + kinetic + gap * speed) + speed * (gap * p * inverse + pressure),
    ]


def three_fluxes(w):
    a = [edge(w[i], w[i + 1], w[i + 2], w[i + 3]) for i in range(5)]
    sides = [states(w[i + 2], a[i], a[i + 1]) for i in range(4)]
    return [hllc(sides[i][0], sides[i + 1][1]) for i in range(3)]


def iotas():
    return (
        lax.broadcasted_iota(jnp.int32, (ROWS, LANES), 0),
        lax.broadcasted_iota(jnp.int32, (ROWS, LANES), 1),
    )


def prolong(value, q):
    row, lane = iotas()
    rows = (q // 2) * 4 + row // 2
    lanes = ((row % 2) * 2 + lane // 64) * 32 + (q % 2) * 16 + (lane % 32) // 2
    return jnp.take_along_axis(jnp.take_along_axis(value, rows, axis=0), lanes, axis=1)


def patch(flux, q):
    row, lane = iotas()
    total = flux + pltpu.roll(flux, LANES - 1, 1)
    total = total + pltpu.roll(total, LANES - 32, 1)
    lanes = ((lane // 32) % 2) * 64 + 2 * (lane % 16)
    rows = 2 * (row % 4) + lane // 64
    placed = jnp.take_along_axis(jnp.take_along_axis(total, lanes, axis=1), rows, axis=0)
    inside = (row // 4 == q // 2) & ((lane % 32) // 16 == q % 2)
    return jnp.where(inside, 0.125 * placed, 0.0)


def single_flux(w):
    a = [edge(w[i], w[i + 1], w[i + 2], w[i + 3]) for i in range(3)]
    upper, _ = states(w[2], a[0], a[1])
    _, lower = states(w[3], a[1], a[2])
    return hllc(upper, lower)


def coarse_ghosts(ref, side, q):
    near, far = (
        primitive([prolong(ref[f, pl.ds(layer, ROWS, stride=2), :], q) for f in range(FIELDS)])
        for layer in range(2)
    )
    return [far, near, near] if side == 0 else [near, near, far]


def edge_planes(cells, block, side, ghosts, store):
    planes = range(5) if side == 0 else range(27, 32)
    inner = [load_plane(cells, block, x) for x in planes]
    w = [primitive(c) for c in inner]
    fluxes = three_fluxes(ghosts + w if side == 0 else w + ghosts)
    for k, i in enumerate((0, 1) if side == 0 else (3, 4)):
        for f in range(FIELDS):
            store(f, planes[i], inner[i][f] - 0.1 * (fluxes[k + 1][f] - fluxes[k][f]))
    return (fluxes[0], fluxes[2]) if side == 0 else (fluxes[2], fluxes[0])


def bulk(cells, out, kept, block):
    first = [load_plane(cells, block, x) for x in range(6)]
    w = [primitive(c) for c in first]
    a = [edge(w[i], w[i + 1], w[i + 2], w[i + 3]) for i in range(3)]
    upper2, _ = states(w[2], a[0], a[1])
    upper3, lower3 = states(w[3], a[1], a[2])
    flux3 = hllc(upper2, lower3)
    for f in range(FIELDS):
        kept[block, 0, f] = flux3[f]

    def step(i, carry):
        w0, w1, w2, low, upper, flux = carry
        w3 = primitive(load_plane(cells, block, i + 2))
        high = edge(w0, w1, w2, w3)
        next_upper, lower = states(w1, low, high)
        next_flux = hllc(upper, lower)
        here = plane_rows(i - 1)
        for f in range(FIELDS):
            out[block, f, here, :] = cells[block, f, here, :] - 0.1 * (next_flux[f] - flux[f])
        return w1, w2, w3, high, next_upper, next_flux

    carry = (w[3], w[4], w[5], a[2], upper3, flux3)
    carry = lax.fori_loop(0, 13, lambda k, c: step(5 + 2 * k, step(4 + 2 * k, c)), carry)
    for f in range(FIELDS):
        kept[block, 1, f] = carry[5][f]


def block_one_edge(side, ghost_planes, cells, kept, store):
    ghosts = [primitive(plane) for plane in ghost_planes]
    _, third = edge_planes(cells, 1, side, ghosts, store)
    x = 2 if side == 0 else 29
    for f in range(FIELDS):
        change = kept[1, 0, f] - third[f] if side == 0 else third[f] - kept[1, 1, f]
        store(f, x, cells[1, f, plane_rows(x), :] - 0.1 * change)


def exchange(
    n_gx, n_gy, links_in, fine, planes, coarse, register,
    out, cells, low_ghosts, kept, faces_out,
    from_below, from_above, links, own_coarse, own_register,
    coarse_below, coarse_above, low_below, high_above, links_below, links_above,
    local_sem, send_sem, recv_sem, relay_sem, beside_sem, below_sem,
):
    gx, gy = lax.axis_index("gx"), lax.axis_index("gy")
    above = (lax.rem(gx + 1, n_gx), gy)
    below = (lax.rem(gx + n_gx - 1, n_gx), gy)
    right = (gx, lax.rem(gy + 1, n_gy))
    left = (gx, lax.rem(gy + n_gy - 1, n_gy))
    odd = lax.rem(gy, 2) == 1
    is_first = gx == 0
    is_last = gx == n_gx - 1

    def fetch(src, dst, k):
        copy = pltpu.make_async_copy(src, dst, local_sem.at[k])
        copy.start()
        return copy

    def signal(semaphore, device):
        pl.semaphore_signal(semaphore, inc=1, device_id=device, device_id_type=MESH)

    barrier = pltpu.get_barrier_semaphore()
    signal(barrier, below)

    @pl.when(odd)
    def _():
        signal(barrier, (below[0], right[1]))

    @pl.when(jnp.logical_not(is_last))
    def _():
        signal(barrier, right)
        signal(barrier, left)

    pl.semaphore_wait(barrier, jnp.where(is_last, 1, 3) + jnp.where(odd, 0, 1))

    def remote(src, dst, device, k, k_send=None):
        return pltpu.make_async_remote_copy(
            src_ref=src, dst_ref=dst, send_sem=send_sem.at[k if k_send is None else k_send],
            recv_sem=recv_sem.at[k], device_id=device, device_id_type=MESH,
        )

    def high(b):
        return planes.at[b, :, 3, :, pl.ds(5, 3)]

    def low(b):
        return planes.at[b, :, 0, :, pl.ds(0, 3)]

    parts = [(0, pl.ds(0, 3)), (0, pl.ds(3, 2)), (1, pl.ds(0, 5))]

    def part(index, column):
        b, fields = parts[index]
        return from_below.at[column, b, fields]

    fine_up = [
        remote(planes.at[b, fields, 3, :, pl.ds(5, 3)], part(k, 1), above, (0, 1, 15)[k], (0, 1, 4)[k])
        for k, (b, fields) in enumerate(parts)
    ]
    coarse_up = remote(coarse.at[0], coarse_below, above, 2, 0)
    low_up = remote(low(0), low_below, above, 3, 1)
    links_up = remote(links_in, links_below, above, 4, 4)
    coarse_down = remote(coarse.at[1], coarse_above, below, 5)
    fine_down = remote(planes.at[:, :, 0, :, pl.ds(0, 3)], from_above.at[1], below, 6)
    high_down = remote(high(0), high_above, below, 7)
    links_down = remote(links_in, links_above, below, 8)
    across_up = remote(high(1), from_below.at[2, 1], (above[0], left[1]), 12)
    on_up = [
        [remote(part(k, 1), part(k, 0), right, r, a), remote(part(k, 1), part(k, 2), left, l, b)]
        for k, (r, l, a, b) in enumerate(((9, 10, 9, 10), (16, 17, 2, 3), (11, 12, 11, 12)))
    ]
    on_down = [
        remote(from_above.at[1], from_above.at[0], right, 13),
        remote(from_above.at[1], from_above.at[2], left, 14),
    ]

    for copy in fine_up:
        copy.start()

    @pl.when(jnp.logical_not(odd))
    def _():
        across_up.start()

    signal(below_sem, above)
    cells_in = [fetch(fine.at[b], cells.at[b], b) for b in range(2)]
    links_copy = fetch(links_in, links, 2)
    coarse_in = fetch(coarse, own_coarse, 3)
    register_in = fetch(register, own_register, 4)
    cells_in[0].wait()
    bulk(cells, out, kept, 0)
    for copy in fine_up:
        copy.wait_send()
    coarse_up.start()
    low_up.start()
    links_up.start()
    cells_in[1].wait()
    bulk(cells, out, kept, 1)

    def forward_down():
        fine_down.wait_recv()
        for copy in on_down:
            copy.start()

    def send_down():
        for copy in (coarse_down, fine_down, high_down, links_down):
            copy.start()

    @pl.when(is_first)
    def _():
        forward_down()

    pl.semaphore_wait(below_sem, 1)
    send_down()

    @pl.when(is_first)
    def _():
        signal(relay_sem.at[0], right)
        signal(relay_sem.at[1], left)

    @pl.when(is_last)
    def _():
        pl.semaphore_wait(beside_sem, 1)

    for k in range(2):
        fine_up[k].wait_recv()
        on_up[k][1].start()
        on_up[k][0].start()
    fine_up[2].wait_recv()
    on_up[2][0].start()

    @pl.when(odd)
    def _():
        on_up[2][1].start()


    @pl.when(is_first)
    def _():
        pl.semaphore_wait(relay_sem.at[0], 1)
        pl.semaphore_wait(relay_sem.at[1], 1)
        signal(beside_sem, below)

    @pl.when(jnp.logical_not(is_first))
    def _():
        forward_down()

    def store(f, x, value):
        out[0, f, plane_rows(x), :] = value

    def block_zero_edge(side):
        ghosts = coarse_ghosts(coarse_above if side == 0 else coarse_below, side, links[0, side, 4])
        _, third = edge_planes(cells, 0, side, ghosts, store)
        x = 2 if side == 0 else 29
        for f in range(FIELDS):
            change = kept[0, 0, f] - third[f] if side == 0 else third[f] - kept[0, 1, f]
            store(f, x, cells[0, f, plane_rows(x), :] - 0.1 * change)

    def coarse_face(t):
        side = 1 - t
        their_links = links_below if side == 0 else links_above
        q = jnp.broadcast_to(their_links[0][side : side + 1, 4:5], (ROWS, LANES))
        outer = low_below if side == 0 else high_above
        ghosts = coarse_ghosts(own_coarse.at[t], side, q)
        w = [primitive(planes_of(outer, x)) for x in range(3)]
        flux = single_flux(ghosts + w if side == 0 else w + ghosts)
        factor = 0.05 if t == 0 else -0.05
        here = pl.ds(t, ROWS, stride=2)
        for f in range(FIELDS):
            faces_out[f, here, :] = own_coarse[t, f, pl.ds(0, ROWS, stride=2), :] + factor * (
                own_register[f, here, :] + patch(flux[f], q)
            )

    def store_one(f, x, value):
        out[1, f, plane_rows(x), :] = value

    links_copy.wait()
    coarse_in.wait()
    register_in.wait()
    coarse_down.wait_recv()
    block_zero_edge(0)
    for copy in (high_down, links_down):
        copy.wait_recv()
    coarse_face(0)
    for copy in on_down:
        copy.wait_recv()
    column, slot = links[1, 1, 2], links[1, 1, 3]
    ghost_planes = [planes_of(from_above.at[column, slot], x) for x in range(3)]
    block_one_edge(1, ghost_planes, cells, kept, store_one)
    coarse_up.wait_recv()
    block_zero_edge(1)
    for copy in (low_up, links_up):
        copy.wait_recv()
    coarse_face(1)

    for copy in (coarse_up, low_up, links_up, coarse_down, fine_down, high_down, links_down):
        copy.wait_send()
    for copy in on_down + on_up[0] + on_up[1] + on_up[2]:
        copy.wait_send()

    for copy in on_up[0] + on_up[1] + on_up[2]:
        copy.wait_recv()
    column, slot = links[1, 0, 2], links[1, 0, 3]
    for x in range(3):
        for f, value in enumerate(planes_of(from_below.at[column, slot], x)):
            low_ghosts[f, x] = value


def finish(done, cells, low_ghosts, kept, faces, out, faces_out, tile, sem):
    def put(src, dst, k):
        copy = pltpu.make_async_copy(src, dst, sem.at[k])
        copy.start()
        return copy

    copies = [
        put(done.at[0], out.at[0], 0),
        put(done.at[1, :, pl.ds(64, 192), :], out.at[1, :, pl.ds(64, 192), :], 1),
        put(faces, faces_out, 2),
    ]

    def store(f, x, value):
        tile[f, pl.ds(x, ROWS, stride=8), :] = value

    ghost_planes = [[low_ghosts[f, x] for f in range(FIELDS)] for x in range(3)]
    block_one_edge(0, ghost_planes, cells, kept, store)
    for f in range(FIELDS):
        for x in range(3, 8):
            store(f, x, done[1, f, plane_rows(x), :])
    copies.append(put(tile, out.at[1, :, pl.ds(0, 64), :], 3))
    for copy in copies:
        copy.wait()


def shards(fine_state, fine_links, coarse_edges, flux_register):
    n_gx, n_gy = lax.axis_size("gx"), lax.axis_size("gy")
    f32 = jnp.float32
    fine = fine_state.reshape(2, FIELDS, 4, 8, 8, LANES).transpose(0, 1, 2, 4, 3, 5)
    planes = fine.reshape(2, FIELDS, 4, 8, 8, 1, LANES)
    fine = fine.reshape(2, FIELDS, 256, LANES)
    coarse = coarse_edges.reshape(2, FIELDS, 2, 8, LANES).transpose(0, 1, 3, 2, 4)
    coarse = coarse.reshape(2, FIELDS, 16, LANES)
    register = flux_register.reshape(2, FIELDS, 8, LANES).transpose(1, 2, 0, 3)
    register = register.reshape(FIELDS, 16, LANES)
    plane = (ROWS, LANES)
    outer = (FIELDS, ROWS, 3, 1, LANES)
    hbm = pl.BlockSpec(memory_space=pltpu.HBM)
    vmem = pl.BlockSpec(memory_space=pltpu.VMEM)
    held = pl.pallas_call(
        lambda *refs: exchange(n_gx, n_gy, *refs),
        out_shape=[
            pltpu.VMEM((2, FIELDS, 256, LANES), f32),
            pltpu.VMEM((2, FIELDS, 256, LANES), f32),
            pltpu.VMEM((FIELDS, 3) + plane, f32),
            pltpu.VMEM((2, 2, FIELDS) + plane, f32),
            pltpu.VMEM((FIELDS, 16, LANES), f32),
        ],
        in_specs=[hbm] * 5,
        out_specs=[vmem] * 5,
        scratch_shapes=[
            pltpu.VMEM((3, 2) + outer, f32),
            pltpu.VMEM((3, 2) + outer, f32),
            pltpu.SMEM((2, 2, 5), jnp.int32),
            pltpu.VMEM((2, FIELDS, 16, LANES), f32),
            pltpu.VMEM((FIELDS, 16, LANES), f32),
            pltpu.VMEM((FIELDS, 16, LANES), f32),
            pltpu.VMEM((FIELDS, 16, LANES), f32),
            pltpu.VMEM(outer, f32),
            pltpu.VMEM(outer, f32),
            pltpu.VMEM((2, 2, 5), jnp.int32),
            pltpu.VMEM((2, 2, 5), jnp.int32),
            pltpu.SemaphoreType.DMA((5,)),
            pltpu.SemaphoreType.DMA((15,)),
            pltpu.SemaphoreType.DMA((18,)),
            pltpu.SemaphoreType.REGULAR((2,)),
            pltpu.SemaphoreType.REGULAR,
            pltpu.SemaphoreType.REGULAR,
        ],
        compiler_params=pltpu.CompilerParams(collective_id=0, has_side_effects=True),
    )(fine_links, fine, planes, coarse, register)
    updated, faces = pl.pallas_call(
        finish,
        out_shape=[
            jax.ShapeDtypeStruct((2, FIELDS, 256, LANES), f32),
            jax.ShapeDtypeStruct((FIELDS, 16, LANES), f32),
        ],
        in_specs=[vmem] * 5,
        out_specs=[hbm, hbm],
        scratch_shapes=[
            pltpu.VMEM((FIELDS, 64, LANES), f32),
            pltpu.SemaphoreType.DMA((4,)),
        ],
        compiler_params=pltpu.CompilerParams(vmem_limit_bytes=8 * 2**20),
    )(*held)
    updated = updated.reshape(2, FIELDS, 4, 8, 8, LANES).transpose(0, 1, 2, 4, 3, 5)
    faces = faces.reshape(1, FIELDS, 8, 2, LANES).transpose(0, 3, 1, 2, 4)
    return (updated.reshape(2, FIELDS, 32, 1024), faces.reshape(1, 2, FIELDS, 1024))


def solution(mesh):
    in_specs = (
        P(("gx", "gy"), None, None, None),
        P(("gx", "gy"), None, None),
        P(("gx", "gy"), None, None, None, None),
        P(("gx", "gy"), None, None, None),
    )
    out_specs = (P(("gx", "gy"), None, None, None), P(("gx", "gy"), None, None, None))
    return jax.shard_map(shards, mesh=mesh, in_specs=in_specs, out_specs=out_specs, check_vma=False)
```
